32 devices in a mesh: tensor: 8 (over y, x, core), dp: 4 (over z).
Axes of the slice: x: 2, y: 2, z: 4, core: 2. Of those that a mesh axis runs over, the one named last changes fastest.
Arguments:
- layer_input: bfloat16 [4, 1024, 3072], P('dp', 'tensor'), may hold values from -6 to 6
- attn_output: bfloat16 [4, 1024, 4096], P('dp', 'tensor'), may hold values from -6 to 6
- grad_gated: bfloat16 [4, 1024, 4096], P('dp', 'tensor'), may hold values from -6 to 6
- gate_weight: bfloat16 [3072, 4096], P(None, 'tensor'), may hold values from -0.109375 to 0.109375
Outputs:
- grad_input: bfloat16 [4, 1024, 3072], P('dp', 'tensor')
- grad_attn: bfloat16 [4, 1024, 4096], P('dp', 'tensor')
- grad_weight: float32 [3072, 4096], P('dp', 'tensor')
The draws below stay inside these ranges and needn't reach their ends.
All inputs are finite; a program needn't handle non-finite values.
Results may differ from the reference program's by a relative error of at most 0.005.
Values may be sent and summed in bfloat16 or wider, within the bound.
No kernel may reach another device: no remote copies, remote signals or barrier semaphores. Data moves between devices by JAX's collectives and lax.ppermute only.
A program may use at most 128 MiB of HBM per device.

```python
import jax
import jax.numpy as jnp
from jax import lax

D = 3072
H = 4096
TOKENS = 1024
REPLICAS = 4


def spiked(drawn, own_key, source, target, blocks, factor):
    def block_of(dim):
        return (jnp.arange(drawn.shape[dim]) // (drawn.shape[dim] // blocks)).reshape((-1,) + (1,) * (drawn.ndim - 1 - dim))

    one_side = jax.random.permutation(own_key, blocks)[block_of(target)]
    far = (block_of(target) + blocks // 2) % blocks
    return jnp.where((block_of(source) == one_side) | (block_of(source) == far), factor * drawn, drawn)


def block_levels(own_key, dims, pieces, least, largest):
    def one(position, blocks):
        draws = jax.random.uniform(jax.random.fold_in(jax.random.fold_in(own_key, 6), position), (blocks,), jnp.float32, least / len(pieces), largest / len(pieces))
        return jnp.repeat(jnp.exp(draws), dims[position] // blocks).reshape((-1,) + (1,) * (len(dims) - position - 1))

    loudness = one(*pieces[0])
    for cut in pieces[1:]:
        loudness = loudness * one(*cut)
    return loudness


def gaussian(rng, dims, spread, bound, shards=(), dtype=jnp.bfloat16):
    level = block_levels(rng, dims, shards, -0.22, 0.18) if shards else 1.0
    entries = jax.random.normal(rng, dims, jnp.float32) * spread * level
    return jnp.minimum(jnp.maximum(entries, -bound), bound).astype(dtype)


def bell_draw_with(stream_key, dims, spread, bound, pieces, heavy, dtype=jnp.bfloat16):
    values = spread * jax.random.normal(stream_key, dims, jnp.float32)
    if pieces:
        values = values * block_levels(stream_key, dims, pieces, -0.22, 0.18)
    return jnp.clip(spiked(values, jax.random.fold_in(stream_key, 3), *heavy), -bound, bound).astype(dtype)


def setup_inputs(seed: int = 0) -> dict:
    splits = jax.random.split(jax.random.key(seed), 5)
    layer_input = bell_draw_with(splits[0], (REPLICAS, TOKENS, D), 1.0, 6.0, ((0, 4), (1, 8)), (0, 2, 4, 2.0))
    attn_output = gaussian(splits[1], (REPLICAS, TOKENS, H), 1.0, 6.0, ((0, 4), (1, 8)))
    grad_gated = gaussian(splits[2], (REPLICAS, TOKENS, H), 1.0, 6.0, ((0, 4), (1, 8)))
    gate_weight = gaussian(splits[3], (D, H), D ** -0.5, 0.109375, ((1, 8),))
    return dict(layer_input=layer_input, attn_output=attn_output, grad_gated=grad_gated, gate_weight=gate_weight)


def reference(layer_input, attn_output, grad_gated, gate_weight):
    flat_input = layer_input.reshape(-1, layer_input.shape[2])
    pre_act = jnp.dot(flat_input, gate_weight, preferred_element_type=jnp.float32)
    gate_val = jax.nn.sigmoid(pre_act)
    cotangent = grad_gated.reshape(-1, grad_gated.shape[2]).astype(jnp.float32)
    attention = attn_output.reshape(-1, attn_output.shape[2]).astype(jnp.float32)
    grad_attn = (cotangent * gate_val).astype(jnp.bfloat16)
    grad_pre = (cotangent * attention * gate_val * (1.0 - gate_val)).astype(jnp.bfloat16)
    grad_input = lax.dot_general(grad_pre, gate_weight, (((1,), (1,)), ((), ())), preferred_element_type=jnp.float32)
    grad_weight = lax.dot_general(flat_input, grad_pre, (((0,), (0,)), ((), ())), preferred_element_type=jnp.float32)
    return (grad_input.astype(jnp.bfloat16).reshape(layer_input.shape),
            grad_attn.reshape(grad_gated.shape),
            grad_weight)
```

```python
import jax
import jax.numpy as jnp
from jax import lax
from jax.sharding import PartitionSpec as P

BF16 = jnp.bfloat16
F32 = jnp.float32


def swap(x, mask):
    count = lax.axis_size("tensor")
    return lax.ppermute(x, "tensor", [(i, i ^ mask) for i in range(count)])


def step_dp(x, by, senders):
    return lax.ppermute(x, "dp", [(i, i + by) for i in senders])


def columns_of(x, chip, core, width):
    own = lax.dynamic_slice_in_dim(x, (2 * chip + core) * width, width, 1)
    other = lax.dynamic_slice_in_dim(x, (2 * chip + 1 - core) * width, width, 1)
    return jnp.concatenate([own, other], 1)


def reduce_over_dp(partial):
    count = lax.axis_size("dp")
    me = lax.axis_index("dp")
    rows = partial.shape[0] // count

    def share(k):
        return lax.dynamic_slice_in_dim(partial, jnp.clip(k, 0, count - 1) * rows, rows, 0)

    right = left = None
    for r in range(1, count):
        to_right, to_left = share(me + count - r), share(me - count + r)
        if r > 1:
            to_right = to_right + right.astype(F32)
            to_left = to_left + left.astype(F32)
        right = step_dp(to_right.astype(BF16), 1, range(0, r))
        left = step_dp(to_left.astype(BF16), -1, range(count - r, count))
    return share(me) + (right.astype(F32) + left.astype(F32)) if count > 1 else share(me)


def on_device(layer_input, attn_output, grad_gated, gate_weight):
    members = lax.axis_size("tensor")
    chips = members // 2
    myself = lax.axis_index("tensor")
    chip, core = myself // 2, myself % 2
    width = gate_weight.shape[1]
    x0 = layer_input[0]
    cot = grad_gated[0]
    att = attn_output[0]

    w_other = swap(gate_weight, 1)
    w_both = jnp.concatenate([gate_weight, w_other], 1)
    xs = [x0] + [swap(x0, 2 * m) for m in range(1, chips)]
    ga = []
    for m in range(chips):
        cols = columns_of(cot, chip ^ m, core, width).astype(F32) * columns_of(att, chip ^ m, core, width).astype(F32)
        cols = cols.astype(BF16)
        ga.append(cols if m == 0 else swap(cols, 2 * m))
    xs_other = [swap(x, 1) for x in xs]

    gates, pres, dxs = [], [], []
    for m in range(chips):
        pre = jnp.dot(xs[m], w_both, preferred_element_type=F32)
        gate = jax.nn.sigmoid(pre)
        gp = (ga[m].astype(F32) * gate * (1.0 - gate)).astype(BF16)
        gate = gate.astype(BF16)
        dx = lax.dot_general(gp, w_both, (((1,), (1,)), ((), ())), preferred_element_type=F32)
        gates.append(gate if m == 0 else swap(gate, 2 * m))
        pres.append(gp)
        dxs.append(dx if m == 0 else swap(dx.astype(BF16), 2 * m))

    gp_all = jnp.concatenate(pres, 0)
    gp_mine = jnp.concatenate([gp_all[:, :width], swap(gp_all[:, width:], 1)], 0)
    x_all = jnp.concatenate(xs + xs_other, 0)
    halves = []
    half = width // 2
    for h in range(2):
        part = lax.dot_general(
            x_all, gp_mine[:, h * half : (h + 1) * half], (((0,), (0,)), ((), ())), preferred_element_type=F32
        )
        halves.append(reduce_over_dp(part))
    grad_weight = jnp.concatenate(halves, 1)

    grad_input = sum(d.astype(F32) for d in dxs).astype(BF16)
    grad_attn = jnp.zeros_like(cot)
    for m in range(chips):
        there = chip ^ m
        for which, cols in ((core, gates[m][:, :width]), (1 - core, gates[m][:, width:])):
            at = (2 * there + which) * width
            piece = lax.dynamic_slice_in_dim(cot, at, width, 1).astype(F32) * cols.astype(F32)
            grad_attn = lax.dynamic_update_slice_in_dim(grad_attn, piece.astype(BF16), at, 1)
    return (grad_input[None], grad_attn[None], grad_weight)


def solution(mesh):
    in_specs = (
        P("dp", "tensor", None),
        P("dp", "tensor", None),
        P("dp", "tensor", None),
        P(None, "tensor"),
    )
    out_specs = (P("dp", "tensor", None), P("dp", "tensor", None), P("dp", "tensor"))
    return jax.shard_map(
        on_device, mesh=mesh, in_specs=in_specs, out_specs=out_specs, check_vma=False
    )
```

```python
import functools

import jax
import jax.numpy as jnp
from jax import lax
from jax.experimental import pallas as pl
from jax.experimental.pallas import tpu as pltpu
from jax.sharding import PartitionSpec as P

BF16 = jnp.bfloat16
F32 = jnp.float32
LIMIT = 24 << 20
ROWS = (((0,), (0,)), ((), ()))
COLUMNS = (((1,), (1,)), ((), ()))


def swap(x, mask):
    count = lax.axis_size("tensor")
    return lax.ppermute(x, "tensor", [(i, i ^ mask) for i in range(count)])


def along_dp(x, pairs):
    return lax.ppermute(x, "dp", pairs)


def tie(*groups):
    return lax.optimization_barrier(groups)


def call(kernel, name, out_shapes, *operands):
    spec = pl.BlockSpec(memory_space=pltpu.VMEM)
    return pl.pallas_call(
        kernel,
        in_specs=[spec] * len(operands),
        out_specs=[spec] * len(out_shapes),
        out_shape=[jax.ShapeDtypeStruct(shape, dtype) for shape, dtype in out_shapes],
        compiler_params=pltpu.CompilerParams(vmem_limit_bytes=LIMIT),
        name=name,
    )(*[pltpu.with_memory_space_constraint(x, pltpu.VMEM) for x in operands])


def stack(refs):
    return jnp.concatenate([ref[...] for ref in refs], 0)


def columns_at(index, width):
    return pl.ds(pl.multiple_of(index * width, width), width)


def chip_columns(m, which, width):
    myself = lax.axis_index("tensor")
    return columns_at(myself ^ (2 * m + which), width)


def product_kernel(width, g_ref, a_ref, *outs):
    for m, out_ref in enumerate(outs):
        for which in range(2):
            cols = chip_columns(m, which, width)
            product = (g_ref[:, cols].astype(F32) * a_ref[:, cols].astype(F32)).astype(BF16)
            out_ref[:, which * width : (which + 1) * width] = product


def products(cot, att, chips, width):
    kernel = functools.partial(product_kernel, width)
    return call(kernel, "products", [((cot.shape[0], 2 * width), BF16)] * chips, cot, att)


def half_kernel(pairs, *refs):
    x_refs, outs = refs[: 2 * pairs], refs[2 * pairs :]
    rows = outs[0].shape[0]
    for i in range(pairs):
        outs[2 * i][...] = x_refs[2 * i][:rows]
        outs[2 * i + 1][...] = x_refs[2 * i + 1][rows:]


def halves(xs):
    shape = (xs[0].shape[0] // 2, xs[0].shape[1])
    return call(functools.partial(half_kernel, len(xs) // 2), "halves", [(shape, BF16)] * len(xs), *xs)


def gate_kernel(xs, gas, *refs):
    x_refs, ga_refs = refs[:xs], refs[xs : xs + gas]
    w_refs, gp_ref, gate_ref = refs[xs + gas : xs + gas + 2], *refs[xs + gas + 2 :]
    x = stack(x_refs)
    width = w_refs[0].shape[1]
    for i, w_ref in enumerate(w_refs):
        cols = slice(i * width, (i + 1) * width)
        gate = jax.nn.sigmoid(jnp.dot(x, w_ref[...], preferred_element_type=F32))
        product = jnp.concatenate([ref[:, cols] for ref in ga_refs], 0).astype(F32)
        gp_ref[:, cols] = (product * gate * (1.0 - gate)).astype(BF16)
        gate_ref[:, cols] = gate.astype(BF16)


def gate_terms(xs, gas, weight, w_other):
    shape = (sum(x.shape[0] for x in xs), 2 * weight.shape[1])
    kernel = functools.partial(gate_kernel, len(xs), len(gas))
    return call(kernel, "gate_terms", [(shape, BF16)] * 2, *xs, *gas, weight, w_other)


def pick(index, table):
    value = jnp.int32(table[-1])
    for i, entry in enumerate(table[:-1]):
        value = jnp.where(index == i, entry, value)
    return value


def share_kernel(tables, rows, xs, *refs):
    x_refs, gp_refs, outs = refs[:xs], refs[xs : -2 * len(tables)], refs[-2 * len(tables) :]
    me = lax.axis_index("dp")
    gp = stack(gp_refs)
    width = outs[0].shape[1]
    for i, table in enumerate(tables):
        cols = columns_at(pick(me, table), rows)
        x = jnp.concatenate([ref[:, cols] for ref in x_refs], 0)
        share = lax.dot_general(x, gp, ROWS, preferred_element_type=F32)
        outs[2 * i][...] = share[:, :width]
        outs[2 * i + 1][...] = share[:, width:].astype(BF16)


def weight_shares(tables, xs, gps, count):
    width = gps[0].shape[1] // 2
    rows = xs[0].shape[1] // count
    shapes = [((rows, width), F32), ((rows, width), BF16)] * len(tables)
    return call(functools.partial(share_kernel, tables, rows, len(xs)), "weight_shares", shapes, *xs, *gps)


def return_kernel(own, gp_ref, gate_ref, w_ref, w_other_ref, *outs):
    width = gp_ref.shape[1] // 2
    tokens = outs[0].shape[0]
    depth = w_ref.shape[0]
    tile = min(depth, 1024)
    for at in range(0, depth, tile):
        rows = slice(at, at + tile)
        dx = lax.dot_general(gp_ref[:, :width], w_ref[rows], COLUMNS, preferred_element_type=F32)
        dx = dx + lax.dot_general(gp_ref[:, width:], w_other_ref[rows], COLUMNS, preferred_element_type=F32)
        for m, out_ref in enumerate(outs):
            out_ref[:, rows] = dx[m * tokens : (m + 1) * tokens].astype(out_ref.dtype)
    for m in range(own, len(outs)):
        outs[m][:, depth:] = gate_ref[m * tokens : (m + 1) * tokens]


def returns_of(own, gp, gate, weight, w_other, tokens):
    depth, width = weight.shape
    chips = gate.shape[0] // tokens
    shapes = [((tokens, depth), F32)] * own + [((tokens, depth + 2 * width), BF16)] * (chips - own)
    return call(functools.partial(return_kernel, own), "returns", shapes, gp, gate, weight, w_other)


def finish_kernel(chips, width, *refs):
    cot_ref, mine_ref, gate_ref = refs[:3]
    back, (input_ref, attn_ref) = refs[3:-2], refs[-2:]
    tokens, depth = mine_ref.shape
    total = mine_ref[...]
    for ref in back:
        total = total + ref[:, :depth].astype(F32)
    input_ref[...] = total.astype(BF16)
    for m in range(chips):
        for which in range(2):
            at = which * width
            gate = back[m - 1][:, depth + at : depth + at + width] if m else gate_ref[:tokens, at : at + width]
            cols = chip_columns(m, which, width)
            attn_ref[:, cols] = (cot_ref[:, cols].astype(F32) * gate.astype(F32)).astype(BF16)


def finish(cot, mine, gate, back, width):
    kernel = functools.partial(finish_kernel, len(back) + 1, width)
    return call(kernel, "finish", [(mine.shape, BF16), (cot.shape, BF16)], cot, mine, gate, *back)


def sum_over_line(share_of, count):
    me = lax.axis_index("dp")
    right = left = None
    for r in range(1, count):
        to_right = share_of(jnp.clip(me + count - r, 0, count - 1))
        to_left = share_of(jnp.clip(me - count + r, 0, count - 1))
        if r > 1:
            to_right = to_right + right.astype(F32)
            to_left = to_left + left.astype(F32)
        right = along_dp(to_right.astype(BF16), [(i, i + 1) for i in range(0, r)])
        left = along_dp(to_left.astype(BF16), [(i, i - 1) for i in range(count - r, count)])
    return share_of(me) + (right.astype(F32) + left.astype(F32))


def on_device(layer_input, attn_output, grad_gated, gate_weight):
    count = lax.axis_size("dp")
    chips = lax.axis_size("tensor") // 2
    depth, width = gate_weight.shape
    tokens = layer_input.shape[1]
    x0 = layer_input[0]
    cot = grad_gated[0]
    near = [1 << bit for bit in range(chips.bit_length() - 1)]
    far = [m for m in range(chips) if m and m not in near]

    xs = {0: [x0]}
    for m in near:
        xs[m] = [swap(x0, 2 * m)]
    w_other = swap(gate_weight, 1)
    ga = products(cot, attn_output[0], chips, width)
    ga, w_other = tie(ga, w_other)
    ga = [swap(piece, 2 * m) if m else piece for m, piece in enumerate(ga)]

    pairs = [m for m in far if (m & (m - 1)) in near]
    held, xs = tie([ga[m] for m in near], xs)
    for m, piece in zip(near, held):
        ga[m] = piece
    if pairs:
        out = halves([xs[bit][0] for m in pairs for bit in (m & -m, m & (m - 1))])
        out, xs = tie(out, xs)
    for m in far:
        if m in pairs:
            i = 2 * pairs.index(m)
            xs[m] = [swap(out[i], 2 * (m & (m - 1))), swap(out[i + 1], 2 * (m & -m))]
        else:
            xs[m] = [swap(x0, 2 * m)]

    def terms_of(some):
        return gate_terms([x for m in some for x in xs[m]], [ga[m] for m in some], gate_weight, w_other)

    first = [0] + near
    gp_near, gate_near = terms_of(first)
    mine, *returns = returns_of(1, gp_near, gate_near, gate_weight, w_other, tokens)
    xs, gp_near, returns = tie(xs, gp_near, returns)
    gps = [gp_near]
    if far:
        gp_far, gate_far = terms_of(far)
        gps.append(gp_far)
    x_list = [x for m in first + far for x in xs[m]]

    back = {m: swap(piece, 2 * m) for m, piece in zip(near, returns)}
    if count == 4:
        rows = depth // count
        own1, other1 = weight_shares([[3, 0, 3, 0]], x_list, gps, count)
        other1, gps = tie(other1, gps)
        other1 = swap(other1, 1)
        own2, other2, own3, other3, own4, other4 = weight_shares(
            [[2, 2, 1, 1], [1, 3, 0, 2], [0, 1, 2, 3]], x_list, gps, count
        )
        other1, other2, other3, other4 = tie(other1, other2, other3, other4)
        other2 = swap(other2, 1)
        message = (own1 + other1.astype(F32)).astype(BF16)
        message, other3, other4 = tie(message, other3, other4)
        ends = along_dp(message, [(0, 1), (1, 0), (2, 3), (3, 2)])
        other3, other4 = swap(other3, 1), swap(other4, 1)
        middle = (own2 + other2.astype(F32)).astype(BF16)
        inner = along_dp(middle, [(1, 2), (2, 1)])
    if far:
        returns = returns_of(0, gp_far, gate_far, gate_weight, w_other, tokens)
    if count == 4:
        kept = own3 + other3.astype(F32)
        own = own4 + other4.astype(F32)
        kept, own, middle, ends, inner, returns, back = tie(
            kept, own, middle, ends, inner, returns, back
        )
        me = lax.axis_index("dp")
        is_end = (me == 0) | (me == count - 1)
        passed = jnp.where(is_end, 0.0, ends.astype(F32))
        message = (kept + passed).astype(BF16)
        own = own + (ends.astype(F32) - passed) + inner.astype(F32)
        message, own, middle, returns = tie(message, own, middle, returns)
        last = along_dp(message, [(0, 1), (1, 3), (2, 0), (3, 2)])
        over = along_dp(middle, [(0, 2), (3, 1)])
    if far:
        back.update({m: swap(piece, 2 * m) for m, piece in zip(far, returns)})
    if count == 4:
        own = own + over.astype(F32)
    grad_input, grad_attn = finish(cot, mine, gate_near, [back[m] for m in range(1, chips)], width)
    if count == 4:
        own, last = tie(own, last)
        grad_weight = own + last.astype(F32)
    else:
        x_all = jnp.concatenate(x_list, 0)
        gp_all = jnp.concatenate(gps, 0)

        def share_of(k):
            cols = lax.dynamic_slice_in_dim(x_all, k * (depth // count), depth // count, 1)
            share = lax.dot_general(cols, gp_all, ROWS, preferred_element_type=F32)
            return share[:, :width] + swap(share[:, width:].astype(BF16), 1).astype(F32)

        grad_weight = sum_over_line(share_of, count)
    return (grad_input[None], grad_attn[None], grad_weight)


def solution(mesh):
    in_specs = (
        P("dp", "tensor", None),
        P("dp", "tensor", None),
        P("dp", "tensor", None),
        P(None, "tensor"),
    )
    out_specs = (P("dp", "tensor", None), P("dp", "tensor", None), P("dp", "tensor"))
    return jax.shard_map(
        on_device, mesh=mesh, in_specs=in_specs, out_specs=out_specs, check_vma=False
    )
```

```python
import functools

import jax
import jax.numpy as jnp
from jax import lax
from jax.experimental import pallas as pl
from jax.experimental.pallas import tpu as pltpu
from jax.sharding import PartitionSpec as P

BF16 = jnp.bfloat16
F32 = jnp.float32
LIMIT = 24 << 20
ROWS = (((0,), (0,)), ((), ()))
COLUMNS = (((1,), (1,)), ((), ()))


def swap(x, mask):
    count = lax.axis_size("tensor")
    return lax.ppermute(x, "tensor", [(i, i ^ mask) for i in range(count)])


def along_dp(x, pairs):
    return lax.ppermute(x, "dp", pairs)


def tie(*groups):
    return lax.optimization_barrier(groups)


def call(kernel, name, out_shapes, *operands):
    spec = pl.BlockSpec(memory_space=pltpu.VMEM)
    return pl.pallas_call(
        kernel,
        in_specs=[spec] * len(operands),
        out_specs=[spec] * len(out_shapes),
        out_shape=[jax.ShapeDtypeStruct(shape, dtype) for shape, dtype in out_shapes],
        compiler_params=pltpu.CompilerParams(vmem_limit_bytes=LIMIT),
        name=name,
    )(*[pltpu.with_memory_space_constraint(x, pltpu.VMEM) for x in operands])


def stack(refs):
    return jnp.concatenate([ref[...] for ref in refs], 0)


def columns_at(index, width):
    return pl.ds(pl.multiple_of(index * width, width), width)


def chip_columns(m, which, width):
    myself = lax.axis_index("tensor")
    return columns_at(myself ^ (2 * m + which), width)


def product_kernel(width, g_ref, a_ref, *outs):
    for m, out_ref in enumerate(outs):
        for which in range(2):
            cols = chip_columns(m, which, width)
            product = (g_ref[:, cols].astype(F32) * a_ref[:, cols].astype(F32)).astype(BF16)
            out_ref[:, which * width : (which + 1) * width] = product


def products(cot, att, chips, width):
    kernel = functools.partial(product_kernel, width)
    return call(kernel, "products", [((cot.shape[0], 2 * width), BF16)] * chips, cot, att)


def half_kernel(pairs, *refs):
    x_refs, outs = refs[: 2 * pairs], refs[2 * pairs :]
    rows = outs[0].shape[0]
    for i in range(pairs):
        outs[2 * i][...] = x_refs[2 * i][:rows]
        outs[2 * i + 1][...] = x_refs[2 * i + 1][rows:]


def halves(xs):
    shape = (xs[0].shape[0] // 2, xs[0].shape[1])
    return call(functools.partial(half_kernel, len(xs) // 2), "halves", [(shape, BF16)] * len(xs), *xs)


def gate_kernel(xs, gas, *refs):
    x_refs, ga_refs = refs[:xs], refs[xs : xs + gas]
    w_refs, gp_ref, gate_ref = refs[xs + gas : xs + gas + 2], *refs[xs + gas + 2 :]
    x = stack(x_refs)
    width = w_refs[0].shape[1]
    for i, w_ref in enumerate(w_refs):
        cols = slice(i * width, (i + 1) * width)
        gate = jax.nn.sigmoid(jnp.dot(x, w_ref[...], preferred_element_type=F32))
        product = jnp.concatenate([ref[:, cols] for ref in ga_refs], 0).astype(F32)
        gp_ref[:, cols] = (product * gate * (1.0 - gate)).astype(BF16)
        gate_ref[:, cols] = gate.astype(BF16)


def gate_terms(xs, gas, weight, w_other):
    shape = (sum(x.shape[0] for x in xs), 2 * weight.shape[1])
    kernel = functools.partial(gate_kernel, len(xs), len(gas))
    return call(kernel, "gate_terms", [(shape, BF16)] * 2, *xs, *gas, weight, w_other)


def pick(index, table):
    value = jnp.int32(table[-1])
    for i, entry in enumerate(table[:-1]):
        value = jnp.where(index == i, entry, value)
    return value


def share_kernel(tables, rows, xs, *refs):
    outs = len(tables) + min(len(tables), 2)
    x_refs, gp_refs, outs = refs[:xs], refs[xs:-outs], refs[-outs:]
    me = lax.axis_index("dp")
    gp = stack(gp_refs)
    width = outs[0].shape[1]
    for i, table in enumerate(tables):
        cols = columns_at(pick(me, table), rows)
        x = jnp.concatenate([ref[:, cols] for ref in x_refs], 0)
        share = lax.dot_general(x, gp, ROWS, preferred_element_type=F32)
        outs[i][...] = share[:, :width]
        at = max(i - 1, 0) * rows
        outs[len(tables) + min(i, 1)][at : at + rows] = share[:, width:].astype(BF16)


def weight_shares(tables, xs, gps, count):
    width = gps[0].shape[1] // 2
    rows = xs[0].shape[1] // count
    shapes = [((rows, width), F32)] * len(tables) + [((rows, width), BF16)]
    if len(tables) > 1:
        shapes.append((((len(tables) - 1) * rows, width), BF16))
    return call(functools.partial(share_kernel, tables, rows, len(xs)), "weight_shares", shapes, *xs, *gps)


def return_kernel(own, gp_ref, gate_ref, w_ref, w_other_ref, *outs):
    width = gp_ref.shape[1] // 2
    depth = w_ref.shape[0]
    tile = min(depth, 1024)
    for at in range(0, depth, tile):
        rows = slice(at, at + tile)
        dx = lax.dot_general(gp_ref[:, :width], w_ref[rows], COLUMNS, preferred_element_type=F32)
        dx = dx + lax.dot_general(gp_ref[:, width:], w_other_ref[rows], COLUMNS, preferred_element_type=F32)
        first = 0
        for out_ref in outs:
            last = first + out_ref.shape[0]
            out_ref[:, rows] = dx[first:last].astype(out_ref.dtype)
            first = last
    first = 0
    for i, out_ref in enumerate(outs):
        last = first + out_ref.shape[0]
        if i >= own:
            out_ref[:, depth:] = gate_ref[first:last]
        first = last


def returns_of(own, gp, gate, weight, w_other, tokens, rows):
    depth, width = weight.shape
    sent = gate.shape[0] - own * tokens
    shapes = [((tokens, depth), F32)] * own + [((rows, depth + 2 * width), BF16)] * (sent // rows)
    return call(functools.partial(return_kernel, own), "returns", shapes, gp, gate, weight, w_other)


def finish_kernel(pieces, width, *refs):
    cot_ref, mine_ref, gate_ref = refs[:3]
    arrived, (input_ref, attn_ref) = refs[3:-2], refs[-2:]
    tokens, depth = mine_ref.shape
    back = []
    for count in pieces:
        back.append(arrived[:count])
        arrived = arrived[count:]

    def read(refs, first, last):
        return jnp.concatenate([ref[:, first:last] for ref in refs], 0).astype(F32)

    total = mine_ref[...]
    for group in back:
        total = total + read(group, 0, depth)
    input_ref[...] = total.astype(BF16)
    for m in range(len(pieces) + 1):
        for which in range(2):
            at = which * width
            if m:
                gate = read(back[m - 1], depth + at, depth + at + width)
            else:
                gate = gate_ref[:tokens, at : at + width].astype(F32)
            cols = chip_columns(m, which, width)
            attn_ref[:, cols] = (cot_ref[:, cols].astype(F32) * gate).astype(BF16)


def finish(cot, mine, gate, back, width):
    kernel = functools.partial(finish_kernel, [len(group) for group in back], width)
    arrived = [piece for group in back for piece in group]
    return call(kernel, "finish", [(mine.shape, BF16), (cot.shape, BF16)], cot, mine, gate, *arrived)


def on_ends(ref, count):
    me = lax.axis_index("dp")
    is_end = (me == 0) | (me == count - 1)
    return jnp.where(is_end, ref[...].astype(F32), 0.0)


def add_kernel(own_ref, other_ref, out_ref):
    out_ref[...] = (own_ref[...] + other_ref[...].astype(F32)).astype(BF16)


def add(own, other):
    return call(add_kernel, "add", [(own.shape, BF16)], own, other)[0]


def pass_kernel(count, own_ref, other_ref, ends_ref, out_ref):
    ends = ends_ref[...].astype(F32) - on_ends(ends_ref, count)
    out_ref[...] = (own_ref[...] + other_ref[: own_ref.shape[0]].astype(F32) + ends).astype(BF16)


def add_passed(own, other, ends, count):
    return call(functools.partial(pass_kernel, count), "add_passed", [(own.shape, BF16)], own, other, ends)[0]


def total_kernel(count, own_ref, other_ref, ends_ref, *refs):
    total = own_ref[...] + other_ref[own_ref.shape[0] :].astype(F32) + on_ends(ends_ref, count)
    for ref in refs[:-1]:
        total = total + ref[...].astype(F32)
    refs[-1][...] = total


def total(own, other, ends, arrived, count):
    kernel = functools.partial(total_kernel, count)
    return call(kernel, "total", [(own.shape, F32)], own, other, ends, *arrived)[0]


def sum_over_line(share_of, count):
    me = lax.axis_index("dp")
    right = left = None
    for r in range(1, count):
        to_right = share_of(jnp.clip(me + count - r, 0, count - 1))
        to_left = share_of(jnp.clip(me - count + r, 0, count - 1))
        if r > 1:
            to_right = to_right + right.astype(F32)
            to_left = to_left + left.astype(F32)
        right = along_dp(to_right.astype(BF16), [(i, i + 1) for i in range(0, r)])
        left = along_dp(to_left.astype(BF16), [(i, i - 1) for i in range(count - r, count)])
    return share_of(me) + (right.astype(F32) + left.astype(F32))


def on_device(layer_input, attn_output, grad_gated, gate_weight):
    count = lax.axis_size("dp")
    chips = lax.axis_size("tensor") // 2
    depth, width = gate_weight.shape
    tokens = layer_input.shape[1]
    x0 = layer_input[0]
    cot = grad_gated[0]
    near = [1 << bit for bit in range(chips.bit_length() - 1)]
    far = [m for m in range(chips) if m and m not in near]

    xs = {0: [x0]}
    for m in near:
        xs[m] = [swap(x0, 2 * m)]
    w_other = swap(gate_weight, 1)
    ga = products(cot, attn_output[0], chips, width)
    ga, w_other = tie(ga, w_other)
    ga = [swap(piece, 2 * m) if m else piece for m, piece in enumerate(ga)]

    pairs = [m for m in far if (m & (m - 1)) in near]
    held, xs = tie([ga[m] for m in near], xs)
    for m, piece in zip(near, held):
        ga[m] = piece
    if pairs:
        out = halves([xs[bit][0] for m in pairs for bit in (m & -m, m & (m - 1))])
        out, xs = tie(out, xs)
    for m in far:
        if m in pairs:
            i = 2 * pairs.index(m)
            xs[m] = [swap(out[i], 2 * (m & (m - 1))), swap(out[i + 1], 2 * (m & -m))]
        else:
            xs[m] = [swap(x0, 2 * m)]

    def terms_of(some):
        return gate_terms([x for m in some for x in xs[m]], [ga[m] for m in some], gate_weight, w_other)

    first = [0] + near
    gp_near, gate_near = terms_of(first)
    mine, *returns = returns_of(1, gp_near, gate_near, gate_weight, w_other, tokens, tokens)
    xs, gp_near, returns = tie(xs, gp_near, returns)
    gps = [gp_near]
    if far:
        gp_far, gate_far = terms_of(far)
        gps.append(gp_far)
    x_list = [x for m in first + far for x in xs[m]]

    back = {m: [swap(piece, 2 * m)] for m, piece in zip(near, returns)}
    if count == 4:
        own1, other1 = weight_shares([[3, 0, 3, 0]], x_list, gps, count)
        other1, gps = tie(other1, gps)
        other1 = swap(other1, 1)
        own2, own3, own4, other2, other34 = weight_shares(
            [[2, 2, 1, 1], [1, 3, 0, 2], [0, 1, 2, 3]], x_list, gps, count
        )
        other2, other34 = swap(other2, 1), swap(other34, 1)
        message = add(own1, other1)
        ends = along_dp(message, [(0, 1), (1, 0), (2, 3), (3, 2)])
        middle = add(own2, other2)
        inner = along_dp(middle, [(1, 2), (2, 1)])
        ends, inner = tie(ends, inner)
        over = along_dp(middle, [(0, 2), (3, 1)])
        message = add_passed(own3, other34, ends, count)
        last = along_dp(message, [(0, 1), (1, 3), (2, 0), (3, 2)])
        message, back, gp_far = tie(message, back, gp_far)
    if far:
        returns = returns_of(0, gp_far, gate_far, gate_weight, w_other, tokens, tokens // 2)
        back.update({m: [swap(piece, 2 * m) for piece in returns[2 * i : 2 * i + 2]] for i, m in enumerate(far)})
    if count == 4:
        grad_weight = total(own4, other34, ends, [inner, over, last], count)
    else:
        x_all = jnp.concatenate(x_list, 0)
        gp_all = jnp.concatenate(gps, 0)

        def share_of(k):
            cols = lax.dynamic_slice_in_dim(x_all, k * (depth // count), depth // count, 1)
            share = lax.dot_general(cols, gp_all, ROWS, preferred_element_type=F32)
            return share[:, :width] + swap(share[:, width:].astype(BF16), 1).astype(F32)

        grad_weight = sum_over_line(share_of, count)
    grad_weight, back, cot = tie(grad_weight, back, cot)
    grad_input, grad_attn = finish(cot, mine, gate_near, [back[m] for m in range(1, chips)], width)
    return (grad_input[None], grad_attn[None], grad_weight)


def solution(mesh):
    in_specs = (
        P("dp", "tensor", None),
        P("dp", "tensor", None),
        P("dp", "tensor", None),
        P(None, "tensor"),
    )
    out_specs = (P("dp", "tensor", None), P("dp", "tensor", None), P("dp", "tensor"))
    return jax.shard_map(
        on_device, mesh=mesh, in_specs=in_specs, out_specs=out_specs, check_vma=False
    )
```

```python
import functools

import jax
import jax.numpy as jnp
from jax import lax
from jax.experimental import pallas as pl
from jax.experimental.pallas import tpu as pltpu
from jax.sharding import PartitionSpec as P

BF16 = jnp.bfloat16
F32 = jnp.float32
LIMIT = 24 << 20
ROWS = (((0,), (0,)), ((), ()))
COLUMNS = (((1,), (1,)), ((), ()))


def swap(x, mask):
    count = lax.axis_size("tensor")
    return lax.ppermute(x, "tensor", [(i, i ^ mask) for i in range(count)])


def along_dp(x, pairs):
    return lax.ppermute(x, "dp", pairs)


def tie(*groups):
    return lax.optimization_barrier(groups)


def call(kernel, name, out_shapes, *operands):
    spec = pl.BlockSpec(memory_space=pltpu.VMEM)
    return pl.pallas_call(
        kernel,
        in_specs=[spec] * len(operands),
        out_specs=[spec] * len(out_shapes),
        out_shape=[jax.ShapeDtypeStruct(shape, dtype) for shape, dtype in out_shapes],
        compiler_params=pltpu.CompilerParams(vmem_limit_bytes=LIMIT),
        name=name,
    )(*[pltpu.with_memory_space_constraint(x, pltpu.VMEM) for x in operands])


def stack(refs):
    return jnp.concatenate([ref[...] for ref in refs], 0)


def columns_at(index, width):
    return pl.ds(pl.multiple_of(index * width, width), width)


def chip_columns(m, which, width):
    myself = lax.axis_index("tensor")
    return columns_at(myself ^ (2 * m + which), width)


def product_kernel(width, g_ref, a_ref, *outs):
    for m, out_ref in enumerate(outs):
        for which in range(2):
            cols = chip_columns(m, which, width)
            product = (g_ref[:, cols].astype(F32) * a_ref[:, cols].astype(F32)).astype(BF16)
            out_ref[:, which * width : (which + 1) * width] = product


def products(cot, att, chips, width):
    kernel = functools.partial(product_kernel, width)
    return call(kernel, "products", [((cot.shape[0], 2 * width), BF16)] * chips, cot, att)


def half_kernel(pairs, *refs):
    x_refs, outs = refs[: 2 * pairs], refs[2 * pairs :]
    rows = outs[0].shape[0]
    for i in range(pairs):
        outs[2 * i][...] = x_refs[2 * i][:rows]
        outs[2 * i + 1][...] = x_refs[2 * i + 1][rows:]


def halves(xs):
    shape = (xs[0].shape[0] // 2, xs[0].shape[1])
    return call(functools.partial(half_kernel, len(xs) // 2), "halves", [(shape, BF16)] * len(xs), *xs)


def gate_kernel(xs, gas, *refs):
    x_refs, ga_refs = refs[:xs], refs[xs : xs + gas]
    w_refs, gp_ref, gate_ref = refs[xs + gas : xs + gas + 2], *refs[xs + gas + 2 :]
    x = stack(x_refs)
    width = w_refs[0].shape[1]
    for i, w_ref in enumerate(w_refs):
        cols = slice(i * width, (i + 1) * width)
        gate = jax.nn.sigmoid(jnp.dot(x, w_ref[...], preferred_element_type=F32))
        product = jnp.concatenate([ref[:, cols] for ref in ga_refs], 0).astype(F32)
        gp_ref[:, cols] = (product * gate * (1.0 - gate)).astype(BF16)
        gate_ref[:, cols] = gate.astype(BF16)


def gate_terms(xs, gas, weight, w_other):
    shape = (sum(x.shape[0] for x in xs), 2 * weight.shape[1])
    kernel = functools.partial(gate_kernel, len(xs), len(gas))
    return call(kernel, "gate_terms", [(shape, BF16)] * 2, *xs, *gas, weight, w_other)


def pick(index, table):
    value = jnp.int32(table[-1])
    for i, entry in enumerate(table[:-1]):
        value = jnp.where(index == i, entry, value)
    return value


def share_kernel(tables, rows, xs, *refs):
    outs = len(tables) + min(len(tables), 2)
    x_refs, gp_refs, outs = refs[:xs], refs[xs:-outs], refs[-outs:]
    me = lax.axis_index("dp")
    gp = stack(gp_refs)
    width = outs[0].shape[1]
    for i, table in enumerate(tables):
        cols = columns_at(pick(me, table), rows)
        x = jnp.concatenate([ref[:, cols] for ref in x_refs], 0)
        share = lax.dot_general(x, gp, ROWS, preferred_element_type=F32)
        outs[i][...] = share[:, :width]
        at = max(i - 1, 0) * rows
        outs[len(tables) + min(i, 1)][at : at + rows] = share[:, width:].astype(BF16)


def weight_shares(tables, xs, gps, count):
    width = gps[0].shape[1] // 2
    rows = xs[0].shape[1] // count
    shapes = [((rows, width), F32)] * len(tables) + [((rows, width), BF16)]
    if len(tables) > 1:
        shapes.append((((len(tables) - 1) * rows, width), BF16))
    return call(functools.partial(share_kernel, tables, rows, len(xs)), "weight_shares", shapes, *xs, *gps)


def return_kernel(own, gp_ref, gate_ref, w_ref, w_other_ref, *outs):
    width = gp_ref.shape[1] // 2
    depth = w_ref.shape[0]
    tile = min(depth, 1024)
    for at in range(0, depth, tile):
        rows = slice(at, at + tile)
        dx = lax.dot_general(gp_ref[:, :width], w_ref[rows], COLUMNS, preferred_element_type=F32)
        dx = dx + lax.dot_general(gp_ref[:, width:], w_other_ref[rows], COLUMNS, preferred_element_type=F32)
        first = 0
        for out_ref in outs:
            last = first + out_ref.shape[0]
            out_ref[:, rows] = dx[first:last].astype(out_ref.dtype)
            first = last
    first = 0
    for i, out_ref in enumerate(outs):
        last = first + out_ref.shape[0]
        if i >= own:
            out_ref[:, depth:] = gate_ref[first:last]
        first = last


def returns_of(own, gp, gate, weight, w_other, tokens, rows):
    depth, width = weight.shape
    sent = gate.shape[0] - own * tokens
    shapes = [((tokens, depth), F32)] * own + [((rows, depth + 2 * width), BF16)] * (sent // rows)
    return call(functools.partial(return_kernel, own), "returns", shapes, gp, gate, weight, w_other)


def finish_kernel(pieces, width, *refs):
    cot_ref, mine_ref, gate_ref = refs[:3]
    arrived, (input_ref, attn_ref) = refs[3:-2], refs[-2:]
    tokens, depth = mine_ref.shape
    back = []
    for count in pieces:
        back.append(arrived[:count])
        arrived = arrived[count:]

    def read(refs, first, last):
        return jnp.concatenate([ref[:, first:last] for ref in refs], 0).astype(F32)

    total = mine_ref[...]
    for group in back:
        total = total + read(group, 0, depth)
    input_ref[...] = total.astype(BF16)
    for m in range(len(pieces) + 1):
        for which in range(2):
            at = which * width
            if m:
                gate = read(back[m - 1], depth + at, depth + at + width)
            else:
                gate = gate_ref[:tokens, at : at + width].astype(F32)
            cols = chip_columns(m, which, width)
            attn_ref[:, cols] = (cot_ref[:, cols].astype(F32) * gate).astype(BF16)


def finish(cot, mine, gate, back, width):
    kernel = functools.partial(finish_kernel, [len(group) for group in back], width)
    arrived = [piece for group in back for piece in group]
    return call(kernel, "finish", [(mine.shape, BF16), (cot.shape, BF16)], cot, mine, gate, *arrived)


def on_ends(ref, count):
    me = lax.axis_index("dp")
    is_end = (me == 0) | (me == count - 1)
    return jnp.where(is_end, ref[...].astype(F32), 0.0)


def add_kernel(own_ref, other_ref, out_ref):
    out_ref[...] = (own_ref[...] + other_ref[...].astype(F32)).astype(BF16)


def add(own, other):
    return call(add_kernel, "add", [(own.shape, BF16)], own, other)[0]


def pass_kernel(count, own_ref, other_ref, ends_ref, out_ref):
    ends = ends_ref[...].astype(F32) - on_ends(ends_ref, count)
    out_ref[...] = (own_ref[...] + other_ref[: own_ref.shape[0]].astype(F32) + ends).astype(BF16)


def add_passed(own, other, ends, count):
    return call(functools.partial(pass_kernel, count), "add_passed", [(own.shape, BF16)], own, other, ends)[0]


def total_kernel(count, own_ref, other_ref, ends_ref, *refs):
    total = own_ref[...] + other_ref[own_ref.shape[0] :].astype(F32) + on_ends(ends_ref, count)
    for ref in refs[:-1]:
        total = total + ref[...].astype(F32)
    refs[-1][...] = total


def total(own, other, ends, arrived, count):
    kernel = functools.partial(total_kernel, count)
    return call(kernel, "total", [(own.shape, F32)], own, other, ends, *arrived)[0]


def sum_over_line(share_of, count):
    me = lax.axis_index("dp")
    right = left = None
    for r in range(1, count):
        to_right = share_of(jnp.clip(me + count - r, 0, count - 1))
        to_left = share_of(jnp.clip(me - count + r, 0, count - 1))
        if r > 1:
            to_right = to_right + right.astype(F32)
            to_left = to_left + left.astype(F32)
        right = along_dp(to_right.astype(BF16), [(i, i + 1) for i in range(0, r)])
        left = along_dp(to_left.astype(BF16), [(i, i - 1) for i in range(count - r, count)])
    return share_of(me) + (right.astype(F32) + left.astype(F32))


def on_device(layer_input, attn_output, grad_gated, gate_weight):
    count = lax.axis_size("dp")
    chips = lax.axis_size("tensor") // 2
    depth, width = gate_weight.shape
    tokens = layer_input.shape[1]
    x0 = layer_input[0]
    cot = grad_gated[0]
    near = [1 << bit for bit in range(chips.bit_length() - 1)]
    far = [m for m in range(chips) if m and m not in near]

    xs = {0: [x0]}
    for m in near:
        xs[m] = [swap(x0, 2 * m)]
    w_other = swap(gate_weight, 1)
    ga = products(cot, attn_output[0], chips, width)
    ga, w_other = tie(ga, w_other)
    ga = [swap(piece, 2 * m) if m else piece for m, piece in enumerate(ga)]

    pairs = [m for m in far if (m & (m - 1)) in near]
    held, xs = tie([ga[m] for m in near], xs)
    for m, piece in zip(near, held):
        ga[m] = piece
    if pairs:
        out = halves([xs[bit][0] for m in pairs for bit in (m & -m, m & (m - 1))])
        out, xs = tie(out, xs)
    for m in far:
        if m in pairs:
            i = 2 * pairs.index(m)
            xs[m] = [swap(out[i], 2 * (m & (m - 1))), swap(out[i + 1], 2 * (m & -m))]
        else:
            xs[m] = [swap(x0, 2 * m)]

    def terms_of(some):
        return gate_terms([x for m in some for x in xs[m]], [ga[m] for m in some], gate_weight, w_other)

    first = [0] + near
    gp_near, gate_near = terms_of(first)
    mine, *returns = returns_of(1, gp_near, gate_near, gate_weight, w_other, tokens, tokens)
    xs, gp_near, returns = tie(xs, gp_near, returns)
    gps = [gp_near]
    if far:
        gp_far, gate_far = terms_of(far)
        gps.append(gp_far)
    x_list = [x for m in first + far for x in xs[m]]

    back = {m: [swap(piece, 2 * m)] for m, piece in zip(near, returns)}
    if count == 4:
        own1, other1 = weight_shares([[3, 0, 3, 0]], x_list, gps, count)
        other1, gps = tie(other1, gps)
        other1 = swap(other1, 1)
        own2, own3, own4, other2, other34 = weight_shares(
            [[2, 2, 1, 1], [1, 3, 0, 2], [0, 1, 2, 3]], x_list, gps, count
        )
        other2, other34 = swap(other2, 1), swap(other34, 1)
        message = add(own1, other1)
        ends = along_dp(message, [(0, 1), (1, 0), (2, 3), (3, 2)])
        middle = add(own2, other2)
        inner = along_dp(middle, [(1, 2), (2, 1)])
        ends, inner = tie(ends, inner)
        over = along_dp(middle, [(0, 2), (3, 1)])
        message = add_passed(own3, other34, ends, count)
        last = along_dp(message, [(0, 1), (1, 3), (2, 0), (3, 2)])
    if far:
        returns = returns_of(0, gp_far, gate_far, gate_weight, w_other, tokens, tokens)
        back.update({m: [swap(piece, 2 * m)] for m, piece in zip(far, returns)})
    grad_input, grad_attn = finish(cot, mine, gate_near, [back[m] for m in range(1, chips)], width)
    if count == 4:
        last, grad_input, grad_attn = tie(last, grad_input, grad_attn)
        grad_weight = total(own4, other34, ends, [inner, over, last], count)
    else:
        x_all = jnp.concatenate(x_list, 0)
        gp_all = jnp.concatenate(gps, 0)

        def share_of(k):
            cols = lax.dynamic_slice_in_dim(x_all, k * (depth // count), depth // count, 1)
            share = lax.dot_general(cols, gp_all, ROWS, preferred_element_type=F32)
            return share[:, :width] + swap(share[:, width:].astype(BF16), 1).astype(F32)

        grad_weight = sum_over_line(share_of, count)
    return (grad_input[None], grad_attn[None], grad_weight)


def solution(mesh):
    in_specs = (
        P("dp", "tensor", None),
        P("dp", "tensor", None),
        P("dp", "tensor", None),
        P(None, "tensor"),
    )
    out_specs = (P("dp", "tensor", None), P("dp", "tensor", None), P("dp", "tensor"))
    return jax.shard_map(
        on_device, mesh=mesh, in_specs=in_specs, out_specs=out_specs, check_vma=False
    )
```

```python
import functools

import jax
import jax.numpy as jnp
from jax import lax
from jax.experimental import pallas as pl
from jax.experimental.pallas import tpu as pltpu
from jax.sharding import PartitionSpec as P

BF16 = jnp.bfloat16
F32 = jnp.float32
LIMIT = 24 << 20
ROWS = (((0,), (0,)), ((), ()))
COLUMNS = (((1,), (1,)), ((), ()))


def swap(x, mask):
    count = lax.axis_size("tensor")
    return lax.ppermute(x, "tensor", [(i, i ^ mask) for i in range(count)])


def along_dp(x, pairs):
    return lax.ppermute(x, "dp", pairs)


def tie(*groups):
    return lax.optimization_barrier(groups)


def call(kernel, name, out_shapes, *operands):
    spec = pl.BlockSpec(memory_space=pltpu.VMEM)
    return pl.pallas_call(
        kernel,
        in_specs=[spec] * len(operands),
        out_specs=[spec] * len(out_shapes),
        out_shape=[jax.ShapeDtypeStruct(shape, dtype) for shape, dtype in out_shapes],
        compiler_params=pltpu.CompilerParams(vmem_limit_bytes=LIMIT),
        name=name,
    )(*[pltpu.with_memory_space_constraint(x, pltpu.VMEM) for x in operands])


def stack(refs):
    return jnp.concatenate([ref[...] for ref in refs], 0)


def columns_at(index, width):
    return pl.ds(pl.multiple_of(index * width, width), width)


def chip_columns(m, which, width):
    myself = lax.axis_index("tensor")
    return columns_at(myself ^ (2 * m + which), width)


def product_kernel(width, g_ref, a_ref, *outs):
    for m, out_ref in enumerate(outs):
        for which in range(2):
            cols = chip_columns(m, which, width)
            product = (g_ref[:, cols].astype(F32) * a_ref[:, cols].astype(F32)).astype(BF16)
            out_ref[:, which * width : (which + 1) * width] = product


def products(cot, att, chips, width):
    kernel = functools.partial(product_kernel, width)
    return call(kernel, "products", [((cot.shape[0], 2 * width), BF16)] * chips, cot, att)


def half_kernel(pairs, *refs):
    x_refs, outs = refs[: 2 * pairs], refs[2 * pairs :]
    rows = outs[0].shape[0]
    for i in range(pairs):
        outs[2 * i][...] = x_refs[2 * i][:rows]
        outs[2 * i + 1][...] = x_refs[2 * i + 1][rows:]


def halves(xs):
    shape = (xs[0].shape[0] // 2, xs[0].shape[1])
    return call(functools.partial(half_kernel, len(xs) // 2), "halves", [(shape, BF16)] * len(xs), *xs)


def gate_kernel(xs, gas, *refs):
    x_refs, ga_refs = refs[:xs], refs[xs : xs + gas]
    w_refs, gp_ref, gate_ref = refs[xs + gas : xs + gas + 2], *refs[xs + gas + 2 :]
    x = stack(x_refs)
    width = w_refs[0].shape[1]
    for i, w_ref in enumerate(w_refs):
        cols = slice(i * width, (i + 1) * width)
        gate = jax.nn.sigmoid(jnp.dot(x, w_ref[...], preferred_element_type=F32))
        product = jnp.concatenate([ref[:, cols] for ref in ga_refs], 0).astype(F32)
        gp_ref[:, cols] = (product * gate * (1.0 - gate)).astype(BF16)
        gate_ref[:, cols] = gate.astype(BF16)


def gate_terms(xs, gas, weight, w_other):
    shape = (sum(x.shape[0] for x in xs), 2 * weight.shape[1])
    kernel = functools.partial(gate_kernel, len(xs), len(gas))
    return call(kernel, "gate_terms", [(shape, BF16)] * 2, *xs, *gas, weight, w_other)


def slope_kernel(xs, *refs):
    w_refs, (gate_ref, slope_ref) = refs[xs : xs + 2], refs[xs + 2 :]
    x = stack(refs[:xs])
    width = w_refs[0].shape[1]
    for i, w_ref in enumerate(w_refs):
        cols = slice(i * width, (i + 1) * width)
        gate = jax.nn.sigmoid(jnp.dot(x, w_ref[...], preferred_element_type=F32))
        gate_ref[:, cols] = gate.astype(BF16)
        slope_ref[:, cols] = gate * (1.0 - gate)


def slope_terms(xs, weight, w_other):
    shape = (sum(x.shape[0] for x in xs), 2 * weight.shape[1])
    return call(functools.partial(slope_kernel, len(xs)), "slope_terms", [(shape, BF16), (shape, F32)], *xs, weight, w_other)


def apply_kernel(*refs):
    ga_refs, (slope_ref, gp_ref, other_ref) = refs[:-3], refs[-3:]
    gp = (stack(ga_refs).astype(F32) * slope_ref[...]).astype(BF16)
    gp_ref[...] = gp
    other_ref[...] = gp[:, other_ref.shape[1] :]


def apply_slope(gas, slope):
    total, width = slope.shape
    return call(apply_kernel, "apply_slope", [((total, width), BF16), ((total, width // 2), BF16)], *gas, slope)


def pick(index, table):
    value = jnp.int32(table[-1])
    for i, entry in enumerate(table[:-1]):
        value = jnp.where(index == i, entry, value)
    return value


def share_kernel(tables, rows, xs, *refs):
    outs = len(tables) + min(len(tables), 2)
    x_refs, gp_refs, outs = refs[:xs], refs[xs:-outs], refs[-outs:]
    me = lax.axis_index("dp")
    gp = stack(gp_refs)
    width = outs[0].shape[1]
    for i, table in enumerate(tables):
        cols = columns_at(pick(me, table), rows)
        x = jnp.concatenate([ref[:, cols] for ref in x_refs], 0)
        share = lax.dot_general(x, gp, ROWS, preferred_element_type=F32)
        outs[i][...] = share[:, :width]
        at = max(i - 1, 0) * rows
        outs[len(tables) + min(i, 1)][at : at + rows] = share[:, width:].astype(BF16)


def weight_shares(tables, xs, gps, count):
    width = gps[0].shape[1] // 2
    rows = xs[0].shape[1] // count
    shapes = [((rows, width), F32)] * len(tables) + [((rows, width), BF16)]
    if len(tables) > 1:
        shapes.append((((len(tables) - 1) * rows, width), BF16))
    return call(functools.partial(share_kernel, tables, rows, len(xs)), "weight_shares", shapes, *xs, *gps)


def far_share(table, rows, x_refs, gp):
    cols = columns_at(pick(lax.axis_index("dp"), table), rows)
    x = jnp.concatenate([ref[:, cols] for ref in x_refs], 0)
    return lax.dot_general(x, gp, ROWS, preferred_element_type=F32)


def first_kernel(table, xs, *refs):
    x_refs, (gp_ref, arrived_ref, own_ref, other_ref, all_ref, message_ref) = refs[:xs], refs[xs:]
    rows, width = own_ref.shape
    half = gp_ref.shape[0]
    all_ref[:half] = gp_ref[:, :width]
    all_ref[half:] = arrived_ref[...]
    share = own_ref[...] + other_ref[...].astype(F32) + far_share(table, rows, x_refs, all_ref[...])
    message_ref[...] = share.astype(BF16)


def first_message(table, xs, gp, arrived, own, other):
    shapes = [((2 * gp.shape[0], own.shape[1]), BF16), (own.shape, BF16)]
    return call(functools.partial(first_kernel, table, len(xs)), "first_message", shapes, *xs, gp, arrived, own, other)


def far_kernel(tables, xs, others, *refs):
    count = len(tables)
    x_refs, gp_ref = refs[:xs], refs[xs]
    owns, other_refs, outs = refs[xs + 1 :][:count], refs[xs + 1 + count :][:others], refs[-count:]
    for i, table in enumerate(tables):
        share = owns[i][...] + far_share(table, owns[i].shape[0], x_refs, gp_ref[...])
        for ref in other_refs:
            share = share + ref[...].astype(F32)
        outs[i][...] = share.astype(outs[i].dtype)


def far_shares(tables, xs, gp, owns, others, dtype):
    shapes = [(own.shape, dtype) for own in owns]
    kernel = functools.partial(far_kernel, tables, len(xs), len(others))
    return call(kernel, "far_shares", shapes, *xs, gp, *owns, *others)


def return_kernel(own, gp_ref, gate_ref, w_ref, w_other_ref, *outs):
    depth, width = w_ref.shape
    tokens = outs[0].shape[0]
    tile = min(depth, 1024)
    for at in range(0, depth, tile):
        rows = slice(at, at + tile)
        dx = lax.dot_general(gp_ref[:, :width], w_ref[rows], COLUMNS, preferred_element_type=F32)
        dx = dx + lax.dot_general(gp_ref[:, width:], w_other_ref[rows], COLUMNS, preferred_element_type=F32)
        for m, out_ref in enumerate(outs):
            out_ref[:, rows] = dx[m * tokens : (m + 1) * tokens].astype(out_ref.dtype)
    for m in range(own, len(outs)):
        outs[m][:, depth:] = gate_ref[m * tokens : (m + 1) * tokens]


def returns_of(own, gp, gate, weight, w_other, tokens):
    depth, width = weight.shape
    chips = gate.shape[0] // tokens
    shapes = [((tokens, depth), F32)] * own + [((tokens, depth + 2 * width), BF16)] * (chips - own)
    return call(functools.partial(return_kernel, own), "returns", shapes, gp, gate, weight, w_other)


def finish_kernel(chips, width, *refs):
    cot_ref, mine_ref, gate_ref = refs[:3]
    back, (input_ref, attn_ref) = refs[3:-2], refs[-2:]
    tokens, depth = mine_ref.shape
    total = mine_ref[...]
    for ref in back:
        total = total + ref[:, :depth].astype(F32)
    input_ref[...] = total.astype(BF16)
    for m in range(chips):
        for which in range(2):
            at = which * width
            gate = back[m - 1][:, depth + at : depth + at + width] if m else gate_ref[:tokens, at : at + width]
            cols = chip_columns(m, which, width)
            attn_ref[:, cols] = (cot_ref[:, cols].astype(F32) * gate.astype(F32)).astype(BF16)


def finish(cot, mine, gate, back, width):
    kernel = functools.partial(finish_kernel, len(back) + 1, width)
    return call(kernel, "finish", [(mine.shape, BF16), (cot.shape, BF16)], cot, mine, gate, *back)


def on_ends(ref, count):
    me = lax.axis_index("dp")
    is_end = (me == 0) | (me == count - 1)
    return jnp.where(is_end, ref[...].astype(F32), 0.0)


def pass_kernel(count, kept_ref, other_ref, ends_ref, out_ref):
    ends = ends_ref[...].astype(F32) - on_ends(ends_ref, count)
    out_ref[...] = (kept_ref[...] + other_ref[...].astype(F32) + ends).astype(BF16)


def add_passed(kept, other, ends, count):
    return call(functools.partial(pass_kernel, count), "add_passed", [(kept.shape, BF16)], kept, other, ends)[0]


def total_kernel(count, own_ref, ends_ref, *refs):
    total = own_ref[...] + on_ends(ends_ref, count)
    for ref in refs[:-1]:
        total = total + ref[...].astype(F32)
    refs[-1][...] = total


def total(own, ends, arrived, count):
    kernel = functools.partial(total_kernel, count)
    return call(kernel, "total", [(own.shape, F32)], own, ends, *arrived)[0]


def sum_over_line(share_of, count):
    me = lax.axis_index("dp")
    right = left = None
    for r in range(1, count):
        to_right = share_of(jnp.clip(me + count - r, 0, count - 1))
        to_left = share_of(jnp.clip(me - count + r, 0, count - 1))
        if r > 1:
            to_right = to_right + right.astype(F32)
            to_left = to_left + left.astype(F32)
        right = along_dp(to_right.astype(BF16), [(i, i + 1) for i in range(0, r)])
        left = along_dp(to_left.astype(BF16), [(i, i - 1) for i in range(count - r, count)])
    return share_of(me) + (right.astype(F32) + left.astype(F32))


def on_device(layer_input, attn_output, grad_gated, gate_weight):
    count = lax.axis_size("dp")
    chips = lax.axis_size("tensor") // 2
    depth, width = gate_weight.shape
    tokens = layer_input.shape[1]
    x0 = layer_input[0]
    cot = grad_gated[0]
    near = [1 << bit for bit in range(chips.bit_length() - 1)]
    far = [m for m in range(chips) if m and m not in near]

    first = [0] + near
    xs = {0: [x0]}
    for m in near:
        xs[m] = [swap(x0, 2 * m)]
    w_other = swap(gate_weight, 1)
    ga = products(cot, attn_output[0], chips, width)
    ga, w_other = tie(ga, w_other)
    ga_near = {m: swap(ga[m], 2 * m) if m else ga[0] for m in first}

    pairs = [m for m in far if (m & (m - 1)) in near]
    ga_near, xs = tie(ga_near, xs)
    if pairs:
        out = halves([xs[bit][0] for m in pairs for bit in (m & -m, m & (m - 1))])
        out, xs = tie(out, xs)
    for m in far:
        if m in pairs:
            i = 2 * pairs.index(m)
            xs[m] = [swap(out[i], 2 * (m & (m - 1))), swap(out[i + 1], 2 * (m & -m))]
        else:
            xs[m] = [swap(x0, 2 * m)]
    ga_far = [swap(ga[m], 2 * m) for m in far]

    x_first = [xs[m][0] for m in first]
    gp_first, gate_first = gate_terms(x_first, [ga_near[m] for m in first], gate_weight, w_other)
    if count == 4:
        to_end, to_middle, passed_on, kept_here = [3, 0, 3, 0], [2, 2, 1, 1], [1, 3, 0, 2], [0, 1, 2, 3]
        own1, other1 = weight_shares([to_end], x_first, [gp_first], count)
        other1, gp_first = tie(other1, gp_first)
        own2, other2 = weight_shares([to_middle], x_first, [gp_first], count)
        other1, other2 = swap(other1, 1), swap(other2, 1)
        own3, own4, other3, other4 = weight_shares([passed_on, kept_here], x_first, [gp_first], count)
        other3, other4 = swap(other3, 1), swap(other4, 1)
    mine, *returns = returns_of(1, gp_first, gate_first, gate_weight, w_other, tokens)
    xs, returns = tie(xs, returns)
    back = {m: swap(piece, 2 * m) for m, piece in zip(near, returns)}

    if far:
        x_far = [x for m in far for x in xs[m]]
        gate_far, slope = slope_terms(x_far, gate_weight, w_other)
        x_far = x_far + [swap(x, 1) for x in x_far]
        gp_far, gp_sent = apply_slope(ga_far, slope)
        gp_arrived = swap(gp_sent, 1)
    if count == 4 and far:
        gp_all, message = first_message(to_end, x_far, gp_far, gp_arrived, own1, other1)
        ends = along_dp(message, [(0, 1), (1, 0), (2, 3), (3, 2)])
        (middle,) = far_shares([to_middle], x_far, gp_all, [own2], [other2], BF16)
        inner = along_dp(middle, [(1, 2), (2, 1)])
        middle, own3, own4, gp_far, gp_all = tie(middle, own3, own4, gp_far, gp_all)
        kept, own = far_shares([passed_on, kept_here], x_far, gp_all, [own3, own4], [], F32)
        ends, inner, kept = tie(ends, inner, kept)
        over = along_dp(middle, [(0, 2), (3, 1)])
        last = along_dp(add_passed(kept, other3, ends, count), [(0, 1), (1, 3), (2, 0), (3, 2)])
    if far:
        returns = returns_of(0, gp_far, gate_far, gate_weight, w_other, tokens)
        back.update({m: swap(piece, 2 * m) for m, piece in zip(far, returns)})
    grad_input, grad_attn = finish(cot, mine, gate_first, [back[m] for m in range(1, chips)], width)
    if count == 4 and far:
        last, grad_input, grad_attn = tie(last, grad_input, grad_attn)
        grad_weight = total(own, ends, [other4, inner, over, last], count)
    else:
        rows = depth // count
        x_first = jnp.concatenate(x_first, 0)
        x_far = jnp.concatenate(x_far, 0) if far else x_first[:0]
        gp_all = jnp.concatenate([gp_far[:, :width], gp_arrived], 0) if far else gp_first[:0, :width]

        def share_of(k):
            def term(x, gp):
                cols = lax.dynamic_slice_in_dim(x, k * rows, rows, 1)
                return lax.dot_general(cols, gp, ROWS, preferred_element_type=F32)

            share = term(x_first, gp_first)
            other = swap(share[:, width:].astype(BF16), 1).astype(F32)
            return share[:, :width] + other + term(x_far, gp_all)

        grad_weight = sum_over_line(share_of, count)
    return (grad_input[None], grad_attn[None], grad_weight)


def solution(mesh):
    in_specs = (
        P("dp", "tensor", None),
        P("dp", "tensor", None),
        P("dp", "tensor", None),
        P(None, "tensor"),
    )
    out_specs = (P("dp", "tensor", None), P("dp", "tensor", None), P("dp", "tensor"))
    return jax.shard_map(
        on_device, mesh=mesh, in_specs=in_specs, out_specs=out_specs, check_vma=False
    )
```

```python
import functools

import jax
import jax.numpy as jnp
from jax import lax
from jax.experimental import pallas as pl
from jax.experimental.pallas import tpu as pltpu
from jax.sharding import PartitionSpec as P

BF16 = jnp.bfloat16
F32 = jnp.float32
LIMIT = 24 << 20
ROWS = (((0,), (0,)), ((), ()))
COLUMNS = (((1,), (1,)), ((), ()))


def swap(x, mask):
    count = lax.axis_size("tensor")
    return lax.ppermute(x, "tensor", [(i, i ^ mask) for i in range(count)])


def along_dp(x, pairs):
    return lax.ppermute(x, "dp", pairs)


def tie(*groups):
    return lax.optimization_barrier(groups)


def call(kernel, name, out_shapes, *operands):
    spec = pl.BlockSpec(memory_space=pltpu.VMEM)
    return pl.pallas_call(
        kernel,
        in_specs=[spec] * len(operands),
        out_specs=[spec] * len(out_shapes),
        out_shape=[jax.ShapeDtypeStruct(shape, dtype) for shape, dtype in out_shapes],
        compiler_params=pltpu.CompilerParams(vmem_limit_bytes=LIMIT),
        name=name,
    )(*[pltpu.with_memory_space_constraint(x, pltpu.VMEM) for x in operands])


def stack(refs):
    return jnp.concatenate([ref[...] for ref in refs], 0)


def columns_at(index, width):
    return pl.ds(pl.multiple_of(index * width, width), width)


def chip_columns(m, which, width):
    myself = lax.axis_index("tensor")
    return columns_at(myself ^ (2 * m + which), width)


def product_kernel(width, g_ref, a_ref, *outs):
    for m, out_ref in enumerate(outs):
        for which in range(2):
            cols = chip_columns(m, which, width)
            product = (g_ref[:, cols].astype(F32) * a_ref[:, cols].astype(F32)).astype(BF16)
            out_ref[:, which * width : (which + 1) * width] = product


def products(cot, att, chips, width):
    kernel = functools.partial(product_kernel, width)
    return call(kernel, "products", [((cot.shape[0], 2 * width), BF16)] * chips, cot, att)


def hold_kernel(x_ref, out_ref):
    out_ref[...] = x_ref[...]


def hold(x):
    return call(hold_kernel, "hold", [(x.shape, x.dtype)], x)[0]


def half_kernel(pairs, *refs):
    x_refs, outs = refs[: 2 * pairs], refs[2 * pairs :]
    rows = outs[0].shape[0]
    for i in range(pairs):
        outs[2 * i][...] = x_refs[2 * i][:rows]
        outs[2 * i + 1][...] = x_refs[2 * i + 1][rows:]


def halves(xs):
    shape = (xs[0].shape[0] // 2, xs[0].shape[1])
    return call(functools.partial(half_kernel, len(xs) // 2), "halves", [(shape, BF16)] * len(xs), *xs)


def gate_kernel(xs, gas, *refs):
    x_refs, ga_refs = refs[:xs], refs[xs : xs + gas]
    w_refs, gp_ref, gate_ref = refs[xs + gas : xs + gas + 2], *refs[xs + gas + 2 :]
    x = stack(x_refs)
    width = w_refs[0].shape[1]
    for i, w_ref in enumerate(w_refs):
        cols = slice(i * width, (i + 1) * width)
        gate = jax.nn.sigmoid(jnp.dot(x, w_ref[...], preferred_element_type=F32))
        product = jnp.concatenate([ref[:, cols] for ref in ga_refs], 0).astype(F32)
        gp_ref[:, cols] = (product * gate * (1.0 - gate)).astype(BF16)
        gate_ref[:, cols] = gate.astype(BF16)


def gate_terms(xs, gas, weight, w_other):
    shape = (sum(x.shape[0] for x in xs), 2 * weight.shape[1])
    kernel = functools.partial(gate_kernel, len(xs), len(gas))
    return call(kernel, "gate_terms", [(shape, BF16)] * 2, *xs, *gas, weight, w_other)


def slope_kernel(xs, *refs):
    w_refs, (gate_ref, slope_ref) = refs[xs : xs + 2], refs[xs + 2 :]
    x = stack(refs[:xs])
    width = w_refs[0].shape[1]
    for i, w_ref in enumerate(w_refs):
        cols = slice(i * width, (i + 1) * width)
        gate = jax.nn.sigmoid(jnp.dot(x, w_ref[...], preferred_element_type=F32))
        gate_ref[:, cols] = gate.astype(BF16)
        slope_ref[:, cols] = gate * (1.0 - gate)


def slope_terms(xs, weight, w_other):
    shape = (sum(x.shape[0] for x in xs), 2 * weight.shape[1])
    return call(functools.partial(slope_kernel, len(xs)), "slope_terms", [(shape, BF16), (shape, F32)], *xs, weight, w_other)


def apply_kernel(*refs):
    ga_refs, (slope_ref, gp_ref, other_ref) = refs[:-3], refs[-3:]
    gp = (stack(ga_refs).astype(F32) * slope_ref[...]).astype(BF16)
    gp_ref[...] = gp
    other_ref[...] = gp[:, other_ref.shape[1] :]


def apply_slope(gas, slope):
    total, width = slope.shape
    return call(apply_kernel, "apply_slope", [((total, width), BF16), ((total, width // 2), BF16)], *gas, slope)


def pick(index, table):
    value = jnp.int32(table[-1])
    for i, entry in enumerate(table[:-1]):
        value = jnp.where(index == i, entry, value)
    return value


def share_kernel(tables, rows, xs, *refs):
    outs = len(tables) + min(len(tables), 2)
    x_refs, gp_refs, outs = refs[:xs], refs[xs:-outs], refs[-outs:]
    me = lax.axis_index("dp")
    gp = stack(gp_refs)
    width = outs[0].shape[1]
    for i, table in enumerate(tables):
        cols = columns_at(pick(me, table), rows)
        x = jnp.concatenate([ref[:, cols] for ref in x_refs], 0)
        share = lax.dot_general(x, gp, ROWS, preferred_element_type=F32)
        outs[i][...] = share[:, :width]
        at = max(i - 1, 0) * rows
        outs[len(tables) + min(i, 1)][at : at + rows] = share[:, width:].astype(BF16)


def weight_shares(tables, xs, gps, count):
    width = gps[0].shape[1] // 2
    rows = xs[0].shape[1] // count
    shapes = [((rows, width), F32)] * len(tables) + [((rows, width), BF16)]
    if len(tables) > 1:
        shapes.append((((len(tables) - 1) * rows, width), BF16))
    return call(functools.partial(share_kernel, tables, rows, len(xs)), "weight_shares", shapes, *xs, *gps)


def far_share(table, rows, x_refs, gp):
    cols = columns_at(pick(lax.axis_index("dp"), table), rows)
    x = jnp.concatenate([ref[:, cols] for ref in x_refs], 0)
    return lax.dot_general(x, gp, ROWS, preferred_element_type=F32)


def first_kernel(table, xs, *refs):
    x_refs, (gp_ref, arrived_ref, own_ref, other_ref, all_ref, message_ref) = refs[:xs], refs[xs:]
    rows, width = own_ref.shape
    half = gp_ref.shape[0]
    all_ref[:half] = gp_ref[:, :width]
    all_ref[half:] = arrived_ref[...]
    share = own_ref[...] + other_ref[...].astype(F32) + far_share(table, rows, x_refs, all_ref[...])
    message_ref[...] = share.astype(BF16)


def first_message(table, xs, gp, arrived, own, other):
    shapes = [((2 * gp.shape[0], own.shape[1]), BF16), (own.shape, BF16)]
    return call(functools.partial(first_kernel, table, len(xs)), "first_message", shapes, *xs, gp, arrived, own, other)


def far_kernel(tables, xs, others, *refs):
    count = len(tables)
    x_refs, gp_ref = refs[:xs], refs[xs]
    owns, other_refs, outs = refs[xs + 1 :][:count], refs[xs + 1 + count :][:others], refs[-count:]
    for i, table in enumerate(tables):
        share = owns[i][...] + far_share(table, owns[i].shape[0], x_refs, gp_ref[...])
        for ref in other_refs:
            share = share + ref[...].astype(F32)
        outs[i][...] = share.astype(outs[i].dtype)


def far_shares(tables, xs, gp, owns, others, dtype):
    shapes = [(own.shape, dtype) for own in owns]
    kernel = functools.partial(far_kernel, tables, len(xs), len(others))
    return call(kernel, "far_shares", shapes, *xs, gp, *owns, *others)


def return_kernel(own, gp_ref, gate_ref, w_ref, w_other_ref, *outs):
    depth, width = w_ref.shape
    tokens = outs[0].shape[0]
    tile = min(depth, 1024)
    for at in range(0, depth, tile):
        rows = slice(at, at + tile)
        dx = lax.dot_general(gp_ref[:, :width], w_ref[rows], COLUMNS, preferred_element_type=F32)
        dx = dx + lax.dot_general(gp_ref[:, width:], w_other_ref[rows], COLUMNS, preferred_element_type=F32)
        for m, out_ref in enumerate(outs):
            out_ref[:, rows] = dx[m * tokens : (m + 1) * tokens].astype(out_ref.dtype)
    for m in range(own, len(outs)):
        outs[m][:, depth:] = gate_ref[m * tokens : (m + 1) * tokens]


def returns_of(own, gp, gate, weight, w_other, tokens):
    depth, width = weight.shape
    chips = gate.shape[0] // tokens
    shapes = [((tokens, depth), F32)] * own + [((tokens, depth + 2 * width), BF16)] * (chips - own)
    return call(functools.partial(return_kernel, own), "returns", shapes, gp, gate, weight, w_other)


def finish_kernel(chips, width, *refs):
    cot_ref, mine_ref, gate_ref = refs[:3]
    back, (input_ref, attn_ref) = refs[3:-2], refs[-2:]
    tokens, depth = mine_ref.shape
    total = mine_ref[...]
    for ref in back:
        total = total + ref[:, :depth].astype(F32)
    input_ref[...] = total.astype(BF16)
    for m in range(chips):
        for which in range(2):
            at = which * width
            gate = back[m - 1][:, depth + at : depth + at + width] if m else gate_ref[:tokens, at : at + width]
            cols = chip_columns(m, which, width)
            attn_ref[:, cols] = (cot_ref[:, cols].astype(F32) * gate.astype(F32)).astype(BF16)


def finish(cot, mine, gate, back, width):
    kernel = functools.partial(finish_kernel, len(back) + 1, width)
    return call(kernel, "finish", [(mine.shape, BF16), (cot.shape, BF16)], cot, mine, gate, *back)


def on_ends(ref, count):
    me = lax.axis_index("dp")
    is_end = (me == 0) | (me == count - 1)
    return jnp.where(is_end, ref[...].astype(F32), 0.0)


def pass_kernel(count, kept_ref, other_ref, ends_ref, out_ref):
    ends = ends_ref[...].astype(F32) - on_ends(ends_ref, count)
    out_ref[...] = (kept_ref[...] + other_ref[...].astype(F32) + ends).astype(BF16)


def add_passed(kept, other, ends, count):
    return call(functools.partial(pass_kernel, count), "add_passed", [(kept.shape, BF16)], kept, other, ends)[0]


def total_kernel(count, own_ref, ends_ref, *refs):
    total = own_ref[...] + on_ends(ends_ref, count)
    for ref in refs[:-1]:
        total = total + ref[...].astype(F32)
    refs[-1][...] = total


def total(own, ends, arrived, count):
    kernel = functools.partial(total_kernel, count)
    return call(kernel, "total", [(own.shape, F32)], own, ends, *arrived)[0]


def sum_over_line(share_of, count):
    me = lax.axis_index("dp")
    right = left = None
    for r in range(1, count):
        to_right = share_of(jnp.clip(me + count - r, 0, count - 1))
        to_left = share_of(jnp.clip(me - count + r, 0, count - 1))
        if r > 1:
            to_right = to_right + right.astype(F32)
            to_left = to_left + left.astype(F32)
        right = along_dp(to_right.astype(BF16), [(i, i + 1) for i in range(0, r)])
        left = along_dp(to_left.astype(BF16), [(i, i - 1) for i in range(count - r, count)])
    return share_of(me) + (right.astype(F32) + left.astype(F32))


def on_device(layer_input, attn_output, grad_gated, gate_weight):
    count = lax.axis_size("dp")
    chips = lax.axis_size("tensor") // 2
    depth, width = gate_weight.shape
    tokens = layer_input.shape[1]
    x0 = layer_input[0]
    cot = grad_gated[0]
    near = [1 << bit for bit in range(chips.bit_length() - 1)]
    far = [m for m in range(chips) if m and m not in near]

    first = [0] + near
    xs = {0: [x0]}
    for m in near:
        xs[m] = [swap(x0, 2 * m)]
    w_other = swap(gate_weight, 1)
    ga = products(cot, attn_output[0], chips, width)
    ga, w_other = tie(ga, w_other)
    ga_near = {m: swap(ga[m], 2 * m) if m else ga[0] for m in first}

    pairs = [m for m in far if (m & (m - 1)) in near]
    held = hold(gate_weight)
    ga, xs, gate_weight = tie(ga, xs, held)
    if pairs:
        out = halves([xs[bit][0] for m in pairs for bit in (m & -m, m & (m - 1))])
        out, xs = tie(out, xs)
    for m in far:
        if m in pairs:
            i = 2 * pairs.index(m)
            xs[m] = [swap(out[i], 2 * (m & (m - 1))), swap(out[i + 1], 2 * (m & -m))]
        else:
            xs[m] = [swap(x0, 2 * m)]
    ga_far = [swap(ga[m], 2 * m) for m in far]

    x_first = [xs[m][0] for m in first]
    gp_first, gate_first = gate_terms(x_first, [ga_near[m] for m in first], gate_weight, w_other)
    if count == 4:
        to_end, to_middle, passed_on, kept_here = [3, 0, 3, 0], [2, 2, 1, 1], [1, 3, 0, 2], [0, 1, 2, 3]
        own1, other1 = weight_shares([to_end], x_first, [gp_first], count)
        other1, gp_first = tie(other1, gp_first)
        own2, other2 = weight_shares([to_middle], x_first, [gp_first], count)
        other1, other2 = swap(other1, 1), swap(other2, 1)
        own3, own4, other3, other4 = weight_shares([passed_on, kept_here], x_first, [gp_first], count)
        other3, other4 = swap(other3, 1), swap(other4, 1)
    mine, *returns = returns_of(1, gp_first, gate_first, gate_weight, w_other, tokens)
    back = {m: swap(piece, 2 * m) for m, piece in zip(near, returns)}

    if far:
        x_far = [x for m in far for x in xs[m]]
        x_after, mine = tie(x_far, mine)
        gate_far, slope = slope_terms(x_after, gate_weight, w_other)
        x_far = x_far + [swap(x, 1) for x in x_far]
        gp_far, gp_sent = apply_slope(ga_far, slope)
        gp_arrived = swap(gp_sent, 1)
    if count == 4 and far:
        gp_all, message = first_message(to_end, x_far, gp_far, gp_arrived, own1, other1)
        ends = along_dp(message, [(0, 1), (1, 0), (2, 3), (3, 2)])
        (middle,) = far_shares([to_middle], x_far, gp_all, [own2], [other2], BF16)
        inner = along_dp(middle, [(1, 2), (2, 1)])
        middle, own3, own4, gp_far, gp_all = tie(middle, own3, own4, gp_far, gp_all)
        kept, own = far_shares([passed_on, kept_here], x_far, gp_all, [own3, own4], [], F32)
        kept, gp_far = tie(kept, gp_far)
        ends, inner, kept = tie(ends, inner, kept)
        over = along_dp(middle, [(0, 2), (3, 1)])
        last = along_dp(add_passed(kept, other3, ends, count), [(0, 1), (1, 3), (2, 0), (3, 2)])
    if far:
        returns = returns_of(0, gp_far, gate_far, gate_weight, w_other, tokens)
        back.update({m: swap(piece, 2 * m) for m, piece in zip(far, returns)})
    grad_input, grad_attn = finish(cot, mine, gate_first, [back[m] for m in range(1, chips)], width)
    if count == 4 and far:
        last, grad_input, grad_attn = tie(last, grad_input, grad_attn)
        grad_weight = total(own, ends, [other4, inner, over, last], count)
    else:
        rows = depth // count
        x_first = jnp.concatenate(x_first, 0)
        x_far = jnp.concatenate(x_far, 0) if far else x_first[:0]
        gp_all = jnp.concatenate([gp_far[:, :width], gp_arrived], 0) if far else gp_first[:0, :width]

        def share_of(k):
            def term(x, gp):
                cols = lax.dynamic_slice_in_dim(x, k * rows, rows, 1)
                return lax.dot_general(cols, gp, ROWS, preferred_element_type=F32)

            share = term(x_first, gp_first)
            other = swap(share[:, width:].astype(BF16), 1).astype(F32)
            return share[:, :width] + other + term(x_far, gp_all)

        grad_weight = sum_over_line(share_of, count)
    return (grad_input[None], grad_attn[None], grad_weight)


def solution(mesh):
    in_specs = (
        P("dp", "tensor", None),
        P("dp", "tensor", None),
        P("dp", "tensor", None),
        P(None, "tensor"),
    )
    out_specs = (P("dp", "tensor", None), P("dp", "tensor", None), P("dp", "tensor"))
    return jax.shard_map(
        on_device, mesh=mesh, in_specs=in_specs, out_specs=out_specs, check_vma=False
    )
```

```python
import functools

import jax
import jax.numpy as jnp
from jax import lax
from jax.experimental import pallas as pl
from jax.experimental.pallas import tpu as pltpu
from jax.sharding import PartitionSpec as P

BF16 = jnp.bfloat16
F32 = jnp.float32
LIMIT = 24 << 20
ROWS = (((0,), (0,)), ((), ()))
COLUMNS = (((1,), (1,)), ((), ()))


def swap(x, mask):
    count = lax.axis_size("tensor")
    return lax.ppermute(x, "tensor", [(i, i ^ mask) for i in range(count)])


def along_dp(x, pairs):
    return lax.ppermute(x, "dp", pairs)


def tie(*groups):
    return lax.optimization_barrier(groups)


def call(kernel, name, out_shapes, *operands):
    spec = pl.BlockSpec(memory_space=pltpu.VMEM)
    return pl.pallas_call(
        kernel,
        in_specs=[spec] * len(operands),
        out_specs=[spec] * len(out_shapes),
        out_shape=[jax.ShapeDtypeStruct(shape, dtype) for shape, dtype in out_shapes],
        compiler_params=pltpu.CompilerParams(vmem_limit_bytes=LIMIT),
        name=name,
    )(*[pltpu.with_memory_space_constraint(x, pltpu.VMEM) for x in operands])


def stack(refs):
    return jnp.concatenate([ref[...] for ref in refs], 0)


def columns_at(index, width):
    return pl.ds(pl.multiple_of(index * width, width), width)


def chip_columns(m, which, width):
    myself = lax.axis_index("tensor")
    return columns_at(myself ^ (2 * m + which), width)


def product_kernel(width, g_ref, a_ref, *outs):
    for m, out_ref in enumerate(outs):
        for which in range(2):
            cols = chip_columns(m, which, width)
            product = (g_ref[:, cols].astype(F32) * a_ref[:, cols].astype(F32)).astype(BF16)
            out_ref[:, which * width : (which + 1) * width] = product


def products(cot, att, chips, width):
    kernel = functools.partial(product_kernel, width)
    return call(kernel, "products", [((cot.shape[0], 2 * width), BF16)] * chips, cot, att)


def hold_kernel(x_ref, out_ref):
    out_ref[...] = x_ref[...]


def hold(x):
    return call(hold_kernel, "hold", [(x.shape, x.dtype)], x)[0]


def half_kernel(pairs, *refs):
    x_refs, outs = refs[: 2 * pairs], refs[2 * pairs :]
    rows = outs[0].shape[0]
    for i in range(pairs):
        outs[2 * i][...] = x_refs[2 * i][:rows]
        outs[2 * i + 1][...] = x_refs[2 * i + 1][rows:]


def halves(xs):
    shape = (xs[0].shape[0] // 2, xs[0].shape[1])
    return call(functools.partial(half_kernel, len(xs) // 2), "halves", [(shape, BF16)] * len(xs), *xs)


def gate_kernel(xs, gas, *refs):
    x_refs, ga_refs = refs[:xs], refs[xs : xs + gas]
    w_refs, gp_ref, gate_ref = refs[xs + gas : xs + gas + 2], *refs[xs + gas + 2 :]
    x = stack(x_refs)
    width = w_refs[0].shape[1]
    for i, w_ref in enumerate(w_refs):
        cols = slice(i * width, (i + 1) * width)
        gate = jax.nn.sigmoid(jnp.dot(x, w_ref[...], preferred_element_type=F32))
        product = jnp.concatenate([ref[:, cols] for ref in ga_refs], 0).astype(F32)
        gp_ref[:, cols] = (product * gate * (1.0 - gate)).astype(BF16)
        gate_ref[:, cols] = gate.astype(BF16)


def gate_terms(xs, gas, weight, w_other):
    shape = (sum(x.shape[0] for x in xs), 2 * weight.shape[1])
    kernel = functools.partial(gate_kernel, len(xs), len(gas))
    return call(kernel, "gate_terms", [(shape, BF16)] * 2, *xs, *gas, weight, w_other)


def slope_kernel(xs, *refs):
    w_refs, (gate_ref, slope_ref) = refs[xs : xs + 2], refs[xs + 2 :]
    x = stack(refs[:xs])
    width = w_refs[0].shape[1]
    for i, w_ref in enumerate(w_refs):
        cols = slice(i * width, (i + 1) * width)
        gate = jax.nn.sigmoid(jnp.dot(x, w_ref[...], preferred_element_type=F32))
        gate_ref[:, cols] = gate.astype(BF16)
        slope_ref[:, cols] = gate * (1.0 - gate)


def slope_terms(xs, weight, w_other):
    shape = (sum(x.shape[0] for x in xs), 2 * weight.shape[1])
    return call(functools.partial(slope_kernel, len(xs)), "slope_terms", [(shape, BF16), (shape, F32)], *xs, weight, w_other)


def apply_kernel(*refs):
    ga_refs, (slope_ref, gp_ref, other_ref) = refs[:-3], refs[-3:]
    gp = (stack(ga_refs).astype(F32) * slope_ref[...]).astype(BF16)
    gp_ref[...] = gp
    other_ref[...] = gp[:, other_ref.shape[1] :]


def apply_slope(gas, slope):
    total, width = slope.shape
    return call(apply_kernel, "apply_slope", [((total, width), BF16), ((total, width // 2), BF16)], *gas, slope)


def pick(index, table):
    value = jnp.int32(table[-1])
    for i, entry in enumerate(table[:-1]):
        value = jnp.where(index == i, entry, value)
    return value


def share_kernel(tables, rows, xs, *refs):
    outs = len(tables) + min(len(tables), 2)
    x_refs, gp_refs, outs = refs[:xs], refs[xs:-outs], refs[-outs:]
    me = lax.axis_index("dp")
    gp = stack(gp_refs)
    width = outs[0].shape[1]
    for i, table in enumerate(tables):
        cols = columns_at(pick(me, table), rows)
        x = jnp.concatenate([ref[:, cols] for ref in x_refs], 0)
        share = lax.dot_general(x, gp, ROWS, preferred_element_type=F32)
        outs[i][...] = share[:, :width]
        at = max(i - 1, 0) * rows
        outs[len(tables) + min(i, 1)][at : at + rows] = share[:, width:].astype(BF16)


def weight_shares(tables, xs, gps, count):
    width = gps[0].shape[1] // 2
    rows = xs[0].shape[1] // count
    shapes = [((rows, width), F32)] * len(tables) + [((rows, width), BF16)]
    if len(tables) > 1:
        shapes.append((((len(tables) - 1) * rows, width), BF16))
    return call(functools.partial(share_kernel, tables, rows, len(xs)), "weight_shares", shapes, *xs, *gps)


def far_share(table, rows, x_refs, gp):
    cols = columns_at(pick(lax.axis_index("dp"), table), rows)
    x = jnp.concatenate([ref[:, cols] for ref in x_refs], 0)
    return lax.dot_general(x, gp, ROWS, preferred_element_type=F32)


def first_kernel(tables, xs, *refs):
    count = len(tables)
    x_refs, (gp_ref, arrived_ref), refs = refs[:xs], refs[xs : xs + 2], refs[xs + 2 :]
    owns, others, (all_ref, *outs) = refs[:count], refs[count : 2 * count], refs[2 * count :]
    rows, width = owns[0].shape
    half = gp_ref.shape[0]
    all_ref[:half] = gp_ref[:, :width]
    all_ref[half:] = arrived_ref[...]
    for table, own_ref, other_ref, out_ref in zip(tables, owns, others, outs):
        share = own_ref[...] + other_ref[...].astype(F32) + far_share(table, rows, x_refs, all_ref[...])
        out_ref[...] = share.astype(BF16)


def first_messages(tables, xs, gp, arrived, owns, others):
    shapes = [((2 * gp.shape[0], owns[0].shape[1]), BF16)] + [(own.shape, BF16) for own in owns]
    kernel = functools.partial(first_kernel, tables, len(xs))
    return call(kernel, "first_messages", shapes, *xs, gp, arrived, *owns, *others)


def far_kernel(tables, xs, others, *refs):
    count = len(tables)
    x_refs, gp_ref = refs[:xs], refs[xs]
    owns, other_refs, outs = refs[xs + 1 :][:count], refs[xs + 1 + count :][:others], refs[-count:]
    for i, table in enumerate(tables):
        share = owns[i][...] + far_share(table, owns[i].shape[0], x_refs, gp_ref[...])
        for ref in other_refs:
            share = share + ref[...].astype(F32)
        outs[i][...] = share.astype(outs[i].dtype)


def far_shares(tables, xs, gp, owns, others, dtype):
    shapes = [(own.shape, dtype) for own in owns]
    kernel = functools.partial(far_kernel, tables, len(xs), len(others))
    return call(kernel, "far_shares", shapes, *xs, gp, *owns, *others)


def return_kernel(own, gp_ref, gate_ref, w_ref, w_other_ref, *outs):
    depth, width = w_ref.shape
    tokens = outs[0].shape[0]
    tile = min(depth, 1024)
    for at in range(0, depth, tile):
        rows = slice(at, at + tile)
        dx = lax.dot_general(gp_ref[:, :width], w_ref[rows], COLUMNS, preferred_element_type=F32)
        dx = dx + lax.dot_general(gp_ref[:, width:], w_other_ref[rows], COLUMNS, preferred_element_type=F32)
        for m, out_ref in enumerate(outs):
            out_ref[:, rows] = dx[m * tokens : (m + 1) * tokens].astype(out_ref.dtype)
    for m in range(own, len(outs)):
        outs[m][:, depth:] = gate_ref[m * tokens : (m + 1) * tokens]


def returns_of(own, gp, gate, weight, w_other, tokens):
    depth, width = weight.shape
    chips = gate.shape[0] // tokens
    shapes = [((tokens, depth), F32)] * own + [((tokens, depth + 2 * width), BF16)] * (chips - own)
    return call(functools.partial(return_kernel, own), "returns", shapes, gp, gate, weight, w_other)


def finish_kernel(chips, width, *refs):
    cot_ref, mine_ref, gate_ref = refs[:3]
    back, (input_ref, attn_ref) = refs[3:-2], refs[-2:]
    tokens, depth = mine_ref.shape
    total = mine_ref[...]
    for ref in back:
        total = total + ref[:, :depth].astype(F32)
    input_ref[...] = total.astype(BF16)
    for m in range(chips):
        for which in range(2):
            at = which * width
            gate = back[m - 1][:, depth + at : depth + at + width] if m else gate_ref[:tokens, at : at + width]
            cols = chip_columns(m, which, width)
            attn_ref[:, cols] = (cot_ref[:, cols].astype(F32) * gate.astype(F32)).astype(BF16)


def finish(cot, mine, gate, back, width):
    kernel = functools.partial(finish_kernel, len(back) + 1, width)
    return call(kernel, "finish", [(mine.shape, BF16), (cot.shape, BF16)], cot, mine, gate, *back)


def on_ends(ref, count):
    me = lax.axis_index("dp")
    is_end = (me == 0) | (me == count - 1)
    return jnp.where(is_end, ref[...].astype(F32), 0.0)


def pass_kernel(count, kept_ref, other_ref, ends_ref, out_ref):
    ends = ends_ref[...].astype(F32) - on_ends(ends_ref, count)
    out_ref[...] = (kept_ref[...] + other_ref[...].astype(F32) + ends).astype(BF16)


def add_passed(kept, other, ends, count):
    return call(functools.partial(pass_kernel, count), "add_passed", [(kept.shape, BF16)], kept, other, ends)[0]


def total_kernel(count, own_ref, ends_ref, *refs):
    total = own_ref[...] + on_ends(ends_ref, count)
    for ref in refs[:-1]:
        total = total + ref[...].astype(F32)
    refs[-1][...] = total


def total(own, ends, arrived, count):
    kernel = functools.partial(total_kernel, count)
    return call(kernel, "total", [(own.shape, F32)], own, ends, *arrived)[0]


def sum_over_line(share_of, count):
    me = lax.axis_index("dp")
    right = left = None
    for r in range(1, count):
        to_right = share_of(jnp.clip(me + count - r, 0, count - 1))
        to_left = share_of(jnp.clip(me - count + r, 0, count - 1))
        if r > 1:
            to_right = to_right + right.astype(F32)
            to_left = to_left + left.astype(F32)
        right = along_dp(to_right.astype(BF16), [(i, i + 1) for i in range(0, r)])
        left = along_dp(to_left.astype(BF16), [(i, i - 1) for i in range(count - r, count)])
    return share_of(me) + (right.astype(F32) + left.astype(F32))


def on_device(layer_input, attn_output, grad_gated, gate_weight):
    count = lax.axis_size("dp")
    chips = lax.axis_size("tensor") // 2
    depth, width = gate_weight.shape
    tokens = layer_input.shape[1]
    x0 = layer_input[0]
    cot = grad_gated[0]
    near = [1 << bit for bit in range(chips.bit_length() - 1)]
    far = [m for m in range(chips) if m and m not in near]

    first = [0] + near
    xs = {0: [x0]}
    for m in near:
        xs[m] = [swap(x0, 2 * m)]
    w_other = swap(gate_weight, 1)
    ga = products(cot, attn_output[0], chips, width)
    ga, w_other = tie(ga, w_other)
    ga_near = {m: swap(ga[m], 2 * m) if m else ga[0] for m in first}

    pairs = [m for m in far if (m & (m - 1)) in near]
    held = hold(gate_weight)
    ga, xs, gate_weight, w_other = tie(ga, xs, held, w_other)
    if pairs:
        out = halves([xs[bit][0] for m in pairs for bit in (m & -m, m & (m - 1))])
        out, xs = tie(out, xs)
    for m in far:
        if m in pairs:
            i = 2 * pairs.index(m)
            xs[m] = [swap(out[i], 2 * (m & (m - 1))), swap(out[i + 1], 2 * (m & -m))]
        else:
            xs[m] = [swap(x0, 2 * m)]
    ga_far = [swap(ga[m], 2 * m) for m in far]

    x_first = [xs[m][0] for m in first]
    gp_first, gate_first = gate_terms(x_first, [ga_near[m] for m in first], gate_weight, w_other)
    if count == 4:
        to_end, to_middle, passed_on, kept_here = [3, 0, 3, 0], [2, 2, 1, 1], [1, 3, 0, 2], [0, 1, 2, 3]
        own1, other1 = weight_shares([to_end], x_first, [gp_first], count)
        other1, gp_first = tie(other1, gp_first)
        own2, other2 = weight_shares([to_middle], x_first, [gp_first], count)
        other1, other2 = swap(other1, 1), swap(other2, 1)
        own3, own4, other3, other4 = weight_shares([passed_on, kept_here], x_first, [gp_first], count)
        other3, other4 = swap(other3, 1), swap(other4, 1)
    mine, *returns = returns_of(1, gp_first, gate_first, gate_weight, w_other, tokens)
    back = {m: swap(piece, 2 * m) for m, piece in zip(near, returns)}

    if far:
        x_far = [x for m in far for x in xs[m]]
        x_after, mine = tie(x_far, mine)
        gate_far, slope = slope_terms(x_after, gate_weight, w_other)
        x_far = x_far + [swap(x, 1) for x in x_far]
        gp_far, gp_sent = apply_slope(ga_far, slope)
        gp_arrived = swap(gp_sent, 1)
    if count == 4 and far:
        gp_all, message, middle = first_messages(
            [to_end, to_middle], x_far, gp_far, gp_arrived, [own1, own2], [other1, other2]
        )
        ends = along_dp(message, [(0, 1), (1, 0), (2, 3), (3, 2)])
        inner = along_dp(middle, [(1, 2), (2, 1)])
        middle, own3, own4, gp_far, gp_all = tie(middle, own3, own4, gp_far, gp_all)
        kept, own = far_shares([passed_on, kept_here], x_far, gp_all, [own3, own4], [], F32)
        kept, gp_far = tie(kept, gp_far)
        ends, inner, kept = tie(ends, inner, kept)
        over = along_dp(middle, [(0, 2), (3, 1)])
        last = along_dp(add_passed(kept, other3, ends, count), [(0, 1), (1, 3), (2, 0), (3, 2)])
    if far:
        returns = returns_of(0, gp_far, gate_far, gate_weight, w_other, tokens)
        back.update({m: swap(piece, 2 * m) for m, piece in zip(far, returns)})
    grad_input, grad_attn = finish(cot, mine, gate_first, [back[m] for m in range(1, chips)], width)
    if count == 4 and far:
        last, grad_input, grad_attn = tie(last, grad_input, grad_attn)
        grad_weight = total(own, ends, [other4, inner, over, last], count)
    else:
        rows = depth // count
        x_first = jnp.concatenate(x_first, 0)
        x_far = jnp.concatenate(x_far, 0) if far else x_first[:0]
        gp_all = jnp.concatenate([gp_far[:, :width], gp_arrived], 0) if far else gp_first[:0, :width]

        def share_of(k):
            def term(x, gp):
                cols = lax.dynamic_slice_in_dim(x, k * rows, rows, 1)
                return lax.dot_general(cols, gp, ROWS, preferred_element_type=F32)

            share = term(x_first, gp_first)
            other = swap(share[:, width:].astype(BF16), 1).astype(F32)
            return share[:, :width] + other + term(x_far, gp_all)

        grad_weight = sum_over_line(share_of, count)
    return (grad_input[None], grad_attn[None], grad_weight)


def solution(mesh):
    in_specs = (
        P("dp", "tensor", None),
        P("dp", "tensor", None),
        P("dp", "tensor", None),
        P(None, "tensor"),
    )
    out_specs = (P("dp", "tensor", None), P("dp", "tensor", None), P("dp", "tensor"))
    return jax.shard_map(
        on_device, mesh=mesh, in_specs=in_specs, out_specs=out_specs, check_vma=False
    )
```

```python
import functools

import jax
import jax.numpy as jnp
from jax import lax
from jax.experimental import pallas as pl
from jax.experimental.pallas import tpu as pltpu
from jax.sharding import PartitionSpec as P

BF16 = jnp.bfloat16
F32 = jnp.float32
LIMIT = 24 << 20
ROWS = (((0,), (0,)), ((), ()))
COLUMNS = (((1,), (1,)), ((), ()))


def swap(x, mask):
    count = lax.axis_size("tensor")
    return lax.ppermute(x, "tensor", [(i, i ^ mask) for i in range(count)])


def along_dp(x, pairs):
    return lax.ppermute(x, "dp", pairs)


def tie(*groups):
    return lax.optimization_barrier(groups)


def call(kernel, name, out_shapes, *operands):
    spec = pl.BlockSpec(memory_space=pltpu.VMEM)
    return pl.pallas_call(
        kernel,
        in_specs=[spec] * len(operands),
        out_specs=[spec] * len(out_shapes),
        out_shape=[jax.ShapeDtypeStruct(shape, dtype) for shape, dtype in out_shapes],
        compiler_params=pltpu.CompilerParams(vmem_limit_bytes=LIMIT),
        name=name,
    )(*[pltpu.with_memory_space_constraint(x, pltpu.VMEM) for x in operands])


def stack(refs):
    return jnp.concatenate([ref[...] for ref in refs], 0)


def columns_at(index, width):
    return pl.ds(pl.multiple_of(index * width, width), width)


def chip_columns(m, which, width):
    myself = lax.axis_index("tensor")
    return columns_at(myself ^ (2 * m + which), width)


def product_kernel(width, g_ref, a_ref, *outs):
    for m, out_ref in enumerate(outs):
        for which in range(2):
            cols = chip_columns(m, which, width)
            product = (g_ref[:, cols].astype(F32) * a_ref[:, cols].astype(F32)).astype(BF16)
            out_ref[:, which * width : (which + 1) * width] = product


def products(cot, att, chips, width):
    kernel = functools.partial(product_kernel, width)
    return call(kernel, "products", [((cot.shape[0], 2 * width), BF16)] * chips, cot, att)


def hold_kernel(x_ref, out_ref):
    out_ref[...] = x_ref[...]


def hold(x):
    return call(hold_kernel, "hold", [(x.shape, x.dtype)], x)[0]


def half_kernel(pairs, *refs):
    x_refs, outs = refs[: 2 * pairs], refs[2 * pairs :]
    rows = outs[0].shape[0]
    for i in range(pairs):
        outs[2 * i][...] = x_refs[2 * i][:rows]
        outs[2 * i + 1][...] = x_refs[2 * i + 1][rows:]


def halves(xs):
    shape = (xs[0].shape[0] // 2, xs[0].shape[1])
    return call(functools.partial(half_kernel, len(xs) // 2), "halves", [(shape, BF16)] * len(xs), *xs)


def gate_kernel(xs, gas, *refs):
    x_refs, ga_refs = refs[:xs], refs[xs : xs + gas]
    w_refs, gp_ref, gate_ref = refs[xs + gas : xs + gas + 2], *refs[xs + gas + 2 :]
    x = stack(x_refs)
    width = w_refs[0].shape[1]
    for i, w_ref in enumerate(w_refs):
        cols = slice(i * width, (i + 1) * width)
        gate = jax.nn.sigmoid(jnp.dot(x, w_ref[...], preferred_element_type=F32))
        product = jnp.concatenate([ref[:, cols] for ref in ga_refs], 0).astype(F32)
        gp_ref[:, cols] = (product * gate * (1.0 - gate)).astype(BF16)
        gate_ref[:, cols] = gate.astype(BF16)


def gate_terms(xs, gas, weight, w_other):
    shape = (sum(x.shape[0] for x in xs), 2 * weight.shape[1])
    kernel = functools.partial(gate_kernel, len(xs), len(gas))
    return call(kernel, "gate_terms", [(shape, BF16)] * 2, *xs, *gas, weight, w_other)


def slope_kernel(xs, *refs):
    w_refs, (gate_ref, slope_ref) = refs[xs : xs + 2], refs[xs + 2 :]
    x = stack(refs[:xs])
    width = w_refs[0].shape[1]
    for i, w_ref in enumerate(w_refs):
        cols = slice(i * width, (i + 1) * width)
        gate = jax.nn.sigmoid(jnp.dot(x, w_ref[...], preferred_element_type=F32))
        gate_ref[:, cols] = gate.astype(BF16)
        slope_ref[:, cols] = gate * (1.0 - gate)


def slope_terms(xs, weight, w_other):
    shape = (sum(x.shape[0] for x in xs), 2 * weight.shape[1])
    return call(functools.partial(slope_kernel, len(xs)), "slope_terms", [(shape, BF16), (shape, F32)], *xs, weight, w_other)


def apply_kernel(*refs):
    ga_refs, (slope_ref, gp_ref, other_ref) = refs[:-3], refs[-3:]
    gp = (stack(ga_refs).astype(F32) * slope_ref[...]).astype(BF16)
    gp_ref[...] = gp
    other_ref[...] = gp[:, other_ref.shape[1] :]


def apply_slope(gas, slope):
    total, width = slope.shape
    return call(apply_kernel, "apply_slope", [((total, width), BF16), ((total, width // 2), BF16)], *gas, slope)


def pick(index, table):
    value = jnp.int32(table[-1])
    for i, entry in enumerate(table[:-1]):
        value = jnp.where(index == i, entry, value)
    return value


def share_kernel(tables, rows, xs, *refs):
    outs = len(tables) + min(len(tables), 2)
    x_refs, gp_refs, outs = refs[:xs], refs[xs:-outs], refs[-outs:]
    me = lax.axis_index("dp")
    gp = stack(gp_refs)
    width = outs[0].shape[1]
    for i, table in enumerate(tables):
        cols = columns_at(pick(me, table), rows)
        x = jnp.concatenate([ref[:, cols] for ref in x_refs], 0)
        share = lax.dot_general(x, gp, ROWS, preferred_element_type=F32)
        outs[i][...] = share[:, :width]
        at = max(i - 1, 0) * rows
        outs[len(tables) + min(i, 1)][at : at + rows] = share[:, width:].astype(BF16)


def weight_shares(tables, xs, gps, count):
    width = gps[0].shape[1] // 2
    rows = xs[0].shape[1] // count
    shapes = [((rows, width), F32)] * len(tables) + [((rows, width), BF16)]
    if len(tables) > 1:
        shapes.append((((len(tables) - 1) * rows, width), BF16))
    return call(functools.partial(share_kernel, tables, rows, len(xs)), "weight_shares", shapes, *xs, *gps)


def far_share(table, rows, x_refs, gp):
    cols = columns_at(pick(lax.axis_index("dp"), table), rows)
    x = jnp.concatenate([ref[:, cols] for ref in x_refs], 0)
    return lax.dot_general(x, gp, ROWS, preferred_element_type=F32)


def first_kernel(tables, xs, *refs):
    count = len(tables)
    x_refs, (gp_ref, arrived_ref), refs = refs[:xs], refs[xs : xs + 2], refs[xs + 2 :]
    owns, others, (all_ref, *outs) = refs[:count], refs[count : 2 * count], refs[2 * count :]
    rows, width = owns[0].shape
    half = gp_ref.shape[0]
    all_ref[:half] = gp_ref[:, :width]
    all_ref[half:] = arrived_ref[...]
    for table, own_ref, other_ref, out_ref in zip(tables, owns, others, outs):
        share = own_ref[...] + other_ref[...].astype(F32) + far_share(table, rows, x_refs, all_ref[...])
        out_ref[...] = share.astype(BF16)


def first_messages(tables, xs, gp, arrived, owns, others):
    shapes = [((2 * gp.shape[0], owns[0].shape[1]), BF16)] + [(own.shape, BF16) for own in owns]
    kernel = functools.partial(first_kernel, tables, len(xs))
    return call(kernel, "first_messages", shapes, *xs, gp, arrived, *owns, *others)


def far_kernel(tables, xs, others, *refs):
    count = len(tables)
    x_refs, gp_ref = refs[:xs], refs[xs]
    owns, other_refs, outs = refs[xs + 1 :][:count], refs[xs + 1 + count :][:others], refs[-count:]
    for i, table in enumerate(tables):
        share = owns[i][...] + far_share(table, owns[i].shape[0], x_refs, gp_ref[...])
        for ref in other_refs:
            share = share + ref[...].astype(F32)
        outs[i][...] = share.astype(outs[i].dtype)


def far_shares(tables, xs, gp, owns, others, dtype):
    shapes = [(own.shape, dtype) for own in owns]
    kernel = functools.partial(far_kernel, tables, len(xs), len(others))
    return call(kernel, "far_shares", shapes, *xs, gp, *owns, *others)


def return_kernel(own, gp_ref, gate_ref, w_ref, w_other_ref, *outs):
    depth, width = w_ref.shape
    tokens = outs[0].shape[0]
    tile = min(depth, 1024)
    for at in range(0, depth, tile):
        rows = slice(at, at + tile)
        dx = lax.dot_general(gp_ref[:, :width], w_ref[rows], COLUMNS, preferred_element_type=F32)
        dx = dx + lax.dot_general(gp_ref[:, width:], w_other_ref[rows], COLUMNS, preferred_element_type=F32)
        for m, out_ref in enumerate(outs):
            out_ref[:, rows] = dx[m * tokens : (m + 1) * tokens].astype(out_ref.dtype)
    for m in range(own, len(outs)):
        outs[m][:, depth:] = gate_ref[m * tokens : (m + 1) * tokens]


def returns_of(own, gp, gate, weight, w_other, tokens):
    depth, width = weight.shape
    chips = gate.shape[0] // tokens
    shapes = [((tokens, depth), F32)] * own + [((tokens, depth + 2 * width), BF16)] * (chips - own)
    return call(functools.partial(return_kernel, own), "returns", shapes, gp, gate, weight, w_other)


def finish_kernel(chips, width, *refs):
    cot_ref, mine_ref, gate_ref = refs[:3]
    back, (input_ref, attn_ref) = refs[3:-2], refs[-2:]
    tokens, depth = mine_ref.shape
    total = mine_ref[...]
    for ref in back:
        total = total + ref[:, :depth].astype(F32)
    input_ref[...] = total.astype(BF16)
    for m in range(chips):
        for which in range(2):
            at = which * width
            gate = back[m - 1][:, depth + at : depth + at + width] if m else gate_ref[:tokens, at : at + width]
            cols = chip_columns(m, which, width)
            attn_ref[:, cols] = (cot_ref[:, cols].astype(F32) * gate.astype(F32)).astype(BF16)


def finish(cot, mine, gate, back, width):
    kernel = functools.partial(finish_kernel, len(back) + 1, width)
    return call(kernel, "finish", [(mine.shape, BF16), (cot.shape, BF16)], cot, mine, gate, *back)


def on_ends(value, count):
    me = lax.axis_index("dp")
    is_end = (me == 0) | (me == count - 1)
    return jnp.where(is_end, value.astype(F32), 0.0)


def pass_kernel(count, kept_ref, other_ref, ends_ref, out_ref):
    ends = ends_ref[...].astype(F32) - on_ends(ends_ref[...], count)
    out_ref[...] = (kept_ref[...] + other_ref[...].astype(F32) + ends).astype(BF16)


def add_passed(kept, other, ends, count):
    return call(functools.partial(pass_kernel, count), "add_passed", [(kept.shape, BF16)], kept, other, ends)[0]


def total_kernel(count, parts, own_ref, ends_ref, *refs):
    arrived, (out_ref, sums, sent) = refs[:-3], refs[-3:]
    rows = own_ref.shape[0] // parts
    copies = []
    for i in range(parts):
        block = slice(i * rows, (i + 1) * rows)
        total = own_ref[block] + on_ends(ends_ref[block], count)
        for ref in arrived:
            total = total + ref[block].astype(F32)
        sums[block] = total
        copies.append(pltpu.make_async_copy(sums.at[pl.ds(i * rows, rows)], out_ref.at[pl.ds(i * rows, rows)], sent.at[i]))
        copies[-1].start()
    for copy in copies:
        copy.wait()


def total(own, ends, arrived, count):
    parts = 4
    operands = [pltpu.with_memory_space_constraint(x, pltpu.VMEM) for x in (own, ends, *arrived)]
    return pl.pallas_call(
        functools.partial(total_kernel, count, parts),
        in_specs=[pl.BlockSpec(memory_space=pltpu.VMEM)] * len(operands),
        out_specs=pl.BlockSpec(memory_space=pl.ANY),
        out_shape=jax.ShapeDtypeStruct(own.shape, F32),
        scratch_shapes=[pltpu.VMEM(own.shape, F32), pltpu.SemaphoreType.DMA((parts,))],
        compiler_params=pltpu.CompilerParams(vmem_limit_bytes=LIMIT),
        name="total",
    )(*operands)


def sum_over_line(share_of, count):
    me = lax.axis_index("dp")
    right = left = None
    for r in range(1, count):
        to_right = share_of(jnp.clip(me + count - r, 0, count - 1))
        to_left = share_of(jnp.clip(me - count + r, 0, count - 1))
        if r > 1:
            to_right = to_right + right.astype(F32)
            to_left = to_left + left.astype(F32)
        right = along_dp(to_right.astype(BF16), [(i, i + 1) for i in range(0, r)])
        left = along_dp(to_left.astype(BF16), [(i, i - 1) for i in range(count - r, count)])
    return share_of(me) + (right.astype(F32) + left.astype(F32))


def on_device(layer_input, attn_output, grad_gated, gate_weight):
    count = lax.axis_size("dp")
    chips = lax.axis_size("tensor") // 2
    depth, width = gate_weight.shape
    tokens = layer_input.shape[1]
    x0 = layer_input[0]
    cot = grad_gated[0]
    near = [1 << bit for bit in range(chips.bit_length() - 1)]
    far = [m for m in range(chips) if m and m not in near]

    first = [0] + near
    xs = {0: [x0]}
    for m in near:
        xs[m] = [swap(x0, 2 * m)]
    w_other = swap(gate_weight, 1)
    ga = products(cot, attn_output[0], chips, width)
    ga, w_other = tie(ga, w_other)
    ga_near = {m: swap(ga[m], 2 * m) if m else ga[0] for m in first}

    pairs = [m for m in far if (m & (m - 1)) in near]
    held = hold(gate_weight)
    ga, xs, gate_weight, w_other = tie(ga, xs, held, w_other)
    if pairs:
        out = halves([xs[bit][0] for m in pairs for bit in (m & -m, m & (m - 1))])
        out, xs = tie(out, xs)
    for m in far:
        if m in pairs:
            i = 2 * pairs.index(m)
            xs[m] = [swap(out[i], 2 * (m & (m - 1))), swap(out[i + 1], 2 * (m & -m))]
        else:
            xs[m] = [swap(x0, 2 * m)]
    ga_far = [swap(ga[m], 2 * m) for m in far]

    x_first = [xs[m][0] for m in first]
    gp_first, gate_first = gate_terms(x_first, [ga_near[m] for m in first], gate_weight, w_other)
    if count == 4:
        to_end, to_middle, passed_on, kept_here = [3, 0, 3, 0], [2, 2, 1, 1], [1, 3, 0, 2], [0, 1, 2, 3]
        own1, other1 = weight_shares([to_end], x_first, [gp_first], count)
        other1, gp_first = tie(other1, gp_first)
        own2, other2 = weight_shares([to_middle], x_first, [gp_first], count)
        other1, other2 = swap(other1, 1), swap(other2, 1)
        own3, own4, other3, other4 = weight_shares([passed_on, kept_here], x_first, [gp_first], count)
        other3, other4 = swap(other3, 1), swap(other4, 1)
    mine, *returns = returns_of(1, gp_first, gate_first, gate_weight, w_other, tokens)
    back = {m: swap(piece, 2 * m) for m, piece in zip(near, returns)}

    if far:
        x_far = [x for m in far for x in xs[m]]
        x_after, mine = tie(x_far, mine)
        gate_far, slope = slope_terms(x_after, gate_weight, w_other)
        x_far = x_far + [swap(x, 1) for x in x_far]
        gp_far, gp_sent = apply_slope(ga_far, slope)
        gp_arrived = swap(gp_sent, 1)
    if count == 4 and far:
        gp_all, message, middle = first_messages(
            [to_end, to_middle], x_far, gp_far, gp_arrived, [own1, own2], [other1, other2]
        )
        ends = along_dp(message, [(0, 1), (1, 0), (2, 3), (3, 2)])
        inner = along_dp(middle, [(1, 2), (2, 1)])
        middle, own3, own4, gp_far, gp_all = tie(middle, own3, own4, gp_far, gp_all)
        kept, own = far_shares([passed_on, kept_here], x_far, gp_all, [own3, own4], [], F32)
        kept, gp_far = tie(kept, gp_far)
        ends, inner, kept = tie(ends, inner, kept)
        over = along_dp(middle, [(0, 2), (3, 1)])
        last = along_dp(add_passed(kept, other3, ends, count), [(0, 1), (1, 3), (2, 0), (3, 2)])
    if far:
        returns = returns_of(0, gp_far, gate_far, gate_weight, w_other, tokens)
        back.update({m: swap(piece, 2 * m) for m, piece in zip(far, returns)})
    grad_input, grad_attn = finish(cot, mine, gate_first, [back[m] for m in range(1, chips)], width)
    if count == 4 and far:
        last, grad_input, grad_attn = tie(last, grad_input, grad_attn)
        grad_weight = total(own, ends, [other4, inner, over, last], count)
    else:
        rows = depth // count
        x_first = jnp.concatenate(x_first, 0)
        x_far = jnp.concatenate(x_far, 0) if far else x_first[:0]
        gp_all = jnp.concatenate([gp_far[:, :width], gp_arrived], 0) if far else gp_first[:0, :width]

        def share_of(k):
            def term(x, gp):
                cols = lax.dynamic_slice_in_dim(x, k * rows, rows, 1)
                return lax.dot_general(cols, gp, ROWS, preferred_element_type=F32)

            share = term(x_first, gp_first)
            other = swap(share[:, width:].astype(BF16), 1).astype(F32)
            return share[:, :width] + other + term(x_far, gp_all)

        grad_weight = sum_over_line(share_of, count)
    return (grad_input[None], grad_attn[None], grad_weight)


def solution(mesh):
    in_specs = (
        P("dp", "tensor", None),
        P("dp", "tensor", None),
        P("dp", "tensor", None),
        P(None, "tensor"),
    )
    out_specs = (P("dp", "tensor", None), P("dp", "tensor", None), P("dp", "tensor"))
    return jax.shard_map(
        on_device, mesh=mesh, in_specs=in_specs, out_specs=out_specs, check_vma=False
    )
```
